512 devices in a mesh: blk: 64 (over z, x_hi, core), sub: 8 (over y, x_lo).
Axes of the slice: x: 4 (x_hi: 2, x_lo: 2; x = x_hi * 2 + x_lo), y: 4, z: 16, core: 2. Of those that a mesh axis runs over, the one named last changes fastest.
Arguments:
- features: float32 [12, 256, 8192], P(None, 'sub', 'blk'), may hold values from -6 to 6
- inverse_diag: float32 [6, 6, 256, 8192], P(None, None, 'sub', 'blk'), may hold values from -0.12 to 1, as said below
- couplings: float32 [4, 256, 8192], P(None, 'sub', 'blk'), may hold values from 0.2 to 0.24
- mismatch: float32 [6, 256, 8192], P(None, 'sub', 'blk'), may hold values from -21 to 21
- production: float32 [6, 256, 8192], P(None, 'sub', 'blk'), may hold values from -6 to 6
- weight_in: float32 [128, 12], replicated, may hold values from -1.75 to 1.75
- bias_in: float32 [128], replicated, may hold values from -0.5 to 0.5
- weight_two: float32 [128, 128], replicated, may hold values from -0.5 to 0.5
- bias_two: float32 [128], replicated, may hold values from -0.5 to 0.5
- weight_three: float32 [128, 128], replicated, may hold values from -0.5 to 0.5
- bias_three: float32 [128], replicated, may hold values from -0.5 to 0.5
- weight_four: float32 [128, 128], replicated, may hold values from -0.5 to 0.5
- bias_four: float32 [128], replicated, may hold values from -0.5 to 0.5
- weight_out: float32 [128], replicated, may hold values from -0.5 to 0.5
Outputs:
- adjoint: float32 [6, 256, 8192], P(None, 'sub', 'blk')
- sensitivity: float32 [256, 8192], P('sub', 'blk')
- correction: float32 [256, 8192], P('sub', 'blk')
- grad_weight_in: float32 [128, 12], replicated
- grad_bias_in: float32 [128], replicated
- grad_weight_two: float32 [128, 128], replicated
- grad_bias_two: float32 [128], replicated
- grad_weight_three: float32 [128, 128], replicated
- grad_bias_three: float32 [128], replicated
- grad_weight_four: float32 [128, 128], replicated
- grad_bias_four: float32 [128], replicated
- grad_weight_out: float32 [128], replicated
The draws below stay inside these ranges and needn't reach their ends.
Inputs may be any that keep to these rules, and one draw needn't show every extreme that they name: `inverse_diag`: a cell's 6 by 6 block with diagonal entries between 0.7 and 1.0 and off-diagonal entries of magnitude at most 0.12.
All inputs are finite; a program needn't handle non-finite values.
Results may differ from the reference program's by a relative error of at most 0.0003.
Values sent between devices are 32-bit elements; how exact they have to be, the bound alone decides.
No kernel may reach another device: no remote copies, remote signals or barrier semaphores. Data moves between devices by JAX's collectives and lax.ppermute only.
A program may use at most 64 MiB of HBM per device.

```python
import jax
import jax.numpy as jnp
from jax import lax

NVAR = 6
NFEAT = 12
HID = 128
SWEEPS = 8
NS = 256
NP = 8192


def draw_inverse_diag(key, part):
    key = jax.random.fold_in(key, 12)
    key_off, key_diag = jax.random.split(key)
    off_part = jax.random.uniform(key_off, (NVAR, NVAR, NS, NP), jnp.float32, -0.1, 0.1)
    diag_part = jax.random.uniform(key_diag, (NVAR, NS, NP), jnp.float32, 0.7, 1.0)
    ident = jnp.eye(NVAR, dtype=jnp.float32)[:, :, None, None]
    return off_part * (1.0 - ident) + ident * diag_part[None]


def draw_mismatch(key, part):
    key = jax.random.fold_in(key, 11)
    position = jnp.arange(NP, dtype=jnp.float32) / NP
    scale = jnp.power(3.0, position)
    base = jnp.clip(jax.random.normal(key, (NVAR, NS, NP), jnp.float32), -6.0, 6.0)
    return base * scale[None, None, :]


def shard_levels(own_key, shape, shards, smallest, largest):
    def one(axis_at, blocks):
        heights = jax.random.uniform(jax.random.fold_in(jax.random.fold_in(own_key, 6), axis_at), (blocks,), jnp.float32, smallest / len(shards), largest / len(shards))
        return jnp.repeat(jnp.exp(heights), shape[axis_at] // blocks).reshape((-1,) + (1,) * (len(shape) - axis_at - 1))

    loudness = one(*shards[0])
    for cut in shards[1:]:
        loudness = loudness * one(*cut)
    return loudness


def bell_draw(rng, extent, width, most, pieces=(), kind=jnp.bfloat16):
    gain = shard_levels(rng, extent, pieces, -0.22, 0.18) if pieces else 1.0
    drawn = jax.random.normal(rng, extent, jnp.float32) * width * gain
    return jnp.minimum(jnp.maximum(drawn, -most), most).astype(kind)


def setup_inputs(seed: int = 0) -> dict:
    key_of = jax.random.split(jax.random.key(seed), 15)
    return {
        "features": bell_draw(key_of[0], (NFEAT, NS, NP), 1.0, 6.0, ((1, 8), (2, 64)), jnp.float32),
        "inverse_diag": draw_inverse_diag(jax.random.fold_in(key_of[14], 71), 0),
        "couplings": jnp.clip(0.2 + 0.03999999 * jax.random.uniform(key_of[2], (4, NS, NP), jnp.float32) ** shard_levels(key_of[2], (4, NS, NP), ((1, 8), (2, 64)), -0.2, 0.2), 0.2, 0.24),
        "mismatch": draw_mismatch(jax.random.fold_in(key_of[14], 71), 0),
        "production": bell_draw(key_of[4], (NVAR, NS, NP), 1.0, 6.0, ((1, 8), (2, 64)), jnp.float32),
        "weight_in": bell_draw(key_of[5], (HID, NFEAT), NFEAT ** -0.5, 1.75, (), jnp.float32),
        "bias_in": jnp.clip(jax.random.uniform(key_of[6], (HID,), jnp.float32, -0.5, 0.5), -0.5, 0.5),
        "weight_two": bell_draw(key_of[7], (HID, HID), HID ** -0.5, 0.5, (), jnp.float32),
        "bias_two": jnp.clip(jax.random.uniform(key_of[8], (HID,), jnp.float32, -0.5, 0.5), -0.5, 0.5),
        "weight_three": bell_draw(key_of[9], (HID, HID), HID ** -0.5, 0.5, (), jnp.float32),
        "bias_three": jnp.clip(jax.random.uniform(key_of[10], (HID,), jnp.float32, -0.5, 0.5), -0.5, 0.5),
        "weight_four": bell_draw(key_of[11], (HID, HID), HID ** -0.5, 0.5, (), jnp.float32),
        "bias_four": jnp.clip(jax.random.uniform(key_of[12], (HID,), jnp.float32, -0.5, 0.5), -0.5, 0.5),
        "weight_out": bell_draw(key_of[13], (HID,), HID ** -0.5, 0.5, (), jnp.float32),
    }


EPS = 1e-06
HIGH = lax.Precision.HIGHEST

def sweep(adjoint, inverse_diag, couplings, mismatch):
    upper_side = jnp.pad(adjoint, ((0, 0), (1, 0), (0, 0)))[:, :-1]
    lower_side = jnp.pad(adjoint, ((0, 0), (0, 1), (0, 0)))[:, 1:]
    pitch_low = jnp.roll(adjoint, 1, axis=2)
    pitch_high = jnp.roll(adjoint, -1, axis=2)
    rhs = mismatch + couplings[0] * upper_side + couplings[1] * lower_side
    rhs = rhs + couplings[2] * pitch_low + couplings[3] * pitch_high
    return lax.optimization_barrier(jnp.sum(inverse_diag * rhs[None], axis=1))

def forward(inputs, weights):
    weight_in, bias_in, weight_two, bias_two, weight_three, bias_three, weight_four, bias_four = weights
    layer_one = jnp.tanh(jnp.einsum('ij,jc->ic', weight_in, inputs, precision=HIGH) + bias_in[:, None])
    layer_two = jnp.tanh(jnp.einsum('ij,jc->ic', weight_two, layer_one, precision=HIGH) + bias_two[:, None])
    layer_three = jnp.tanh(jnp.einsum('ij,jc->ic', weight_three, layer_two, precision=HIGH) + bias_three[:, None])
    layer_four = jnp.tanh(jnp.einsum('ij,jc->ic', weight_four, layer_three, precision=HIGH) + bias_four[:, None])
    return (layer_one, layer_two, layer_three, layer_four)

def top_terms(layer_four, layer_three, upstream, weight_out):
    grad_out = jnp.einsum('ic,c->i', layer_four, upstream, precision=HIGH)
    delta_four = weight_out[:, None] * upstream[None, :] * (1.0 - layer_four * layer_four)
    grad_four = jnp.einsum('ic,jc->ij', delta_four, layer_three, precision=HIGH)
    return (grad_out, grad_four, lax.optimization_barrier(jnp.sum(delta_four, axis=1)), delta_four)

def next_terms(delta_next, weight_next, layer_now, layer_prev):
    delta_now = jnp.einsum('ji,jc->ic', weight_next, delta_next, precision=HIGH) * (1.0 - layer_now * layer_now)
    grad_now = jnp.einsum('ic,jc->ij', delta_now, layer_prev, precision=HIGH)
    return (grad_now, lax.optimization_barrier(jnp.sum(delta_now, axis=1)), delta_now)

def reference(features, inverse_diag, couplings, mismatch, production, weight_in, bias_in, weight_two, bias_two, weight_three, bias_three, weight_four, bias_four, weight_out):
    adjoint = jnp.zeros((NVAR, NS, NP), jnp.float32)
    for sweep_index in range(SWEEPS):
        adjoint = sweep(adjoint, inverse_diag, couplings, mismatch)
    sensitivity = -lax.optimization_barrier(jnp.sum(adjoint * production, axis=0))
    norm_value = jnp.sqrt(jnp.sum(sensitivity * sensitivity) + EPS)
    upstream = sensitivity / norm_value
    weights = (weight_in, bias_in, weight_two, bias_two, weight_three, bias_three, weight_four, bias_four)

    def row_step(totals, row):
        inputs, row_up = row
        layer_one, layer_two, layer_three, layer_four = forward(inputs, weights)
        correction_row = 1.0 + jnp.einsum('i,ic->c', weight_out, layer_four, precision=HIGH)
        grad_out, grad_four, gb_four, delta_four = top_terms(layer_four, layer_three, row_up, weight_out)
        grad_three, gb_three, delta_three = next_terms(delta_four, weight_four, layer_three, layer_two)
        grad_two, gb_two, delta_two = next_terms(delta_three, weight_three, layer_two, layer_one)
        grad_one, gb_one, delta_one = next_terms(delta_two, weight_two, layer_one, inputs)
        terms = (grad_one, gb_one, grad_two, gb_two, grad_three, gb_three, grad_four, gb_four, grad_out)
        return (tuple((a + b for a, b in zip(totals, terms))), correction_row)
    zeros_init = (jnp.zeros((HID, NFEAT), jnp.float32), jnp.zeros((HID,), jnp.float32), jnp.zeros((HID, HID), jnp.float32), jnp.zeros((HID,), jnp.float32), jnp.zeros((HID, HID), jnp.float32), jnp.zeros((HID,), jnp.float32), jnp.zeros((HID, HID), jnp.float32), jnp.zeros((HID,), jnp.float32), jnp.zeros((HID,), jnp.float32))
    totals, correction = lax.scan(row_step, zeros_init, (jnp.transpose(features, (1, 0, 2)), upstream))
    return (adjoint, sensitivity, correction, totals[0], totals[1], totals[2], totals[3], totals[4], totals[5], totals[6], totals[7], totals[8])
```

```python
import jax
import jax.numpy as jnp
from jax import lax
from jax.experimental import pallas as pl
from jax.experimental.pallas import tpu as pltpu
from jax.sharding import Mesh, PartitionSpec as P

SWEEPS = 8
EPS = 1e-06
BLK = ("z", "xh", "c")
SUB = ("y", "xl")
NEAR = ("xh", "c", "y", "xl")
FAR = ("z",)
F32 = jnp.float32
BF16 = jnp.bfloat16
GROUP = 4
MIB = 1 << 20


def split(value):
    high = value.astype(BF16)
    return high, (value - high.astype(F32)).astype(BF16)


def pair(value):
    return jnp.concatenate(split(value), axis=1)


def joined(both):
    return both[:, :128].astype(F32) + both[:, 128:].astype(F32)


def times(both, weights):
    out = jnp.dot(both, weights, preferred_element_type=F32)
    return out[:, :128] + out[:, 128:]


def stacked(weight):
    both = pair(weight)
    return jnp.concatenate([both, both], axis=0)


def forward_kernel(x_ref, win_ref, w2_ref, w3_ref, w4_ref, vec_ref,
                   xc_ref, l1_ref, l2_ref, l3_ref, l4_ref, s1, s2, s3, s4):
    @pl.when(pl.program_id(0) == 0)
    def _():
        high, low = split(win_ref[...])
        s1[...] = jnp.concatenate([high, high, low], axis=0)
        for raw, kept in ((w2_ref, s2), (w3_ref, s3), (w4_ref, s4)):
            kept[...] = stacked(raw[...].T)

    columns = []
    for r in range(GROUP):
        x = x_ref[r]
        high = x.astype(BF16).astype(F32)
        column = jnp.concatenate([high, x - high, high], axis=0).T.astype(BF16)
        xc_ref[r] = column
        columns.append(column)
    inputs = jnp.concatenate(columns, axis=0)
    layer = jnp.tanh(jnp.dot(inputs, s1[...], preferred_element_type=F32) + vec_ref[0:1])
    for k, (out, weights) in enumerate(((l1_ref, s2), (l2_ref, s3), (l3_ref, s4))):
        both = pair(layer)
        out[...] = both.reshape(GROUP, 128, 256)
        layer = jnp.tanh(times(both, weights[...]) + vec_ref[k + 1 : k + 2])
    l4_ref[...] = layer.reshape(GROUP, 128, 128)


def forward_call(x, win, w2, w3, w4, vec, rows):
    whole = lambda shape: pl.BlockSpec(shape, lambda i: (0, 0))
    block = lambda a, b: pl.BlockSpec((GROUP, a, b), lambda i: (i, 0, 0))
    return pl.pallas_call(
        forward_kernel,
        grid=(rows // GROUP,),
        in_specs=[block(16, 128), whole((16, 128))] + [whole((128, 128))] * 3 + [whole((8, 128))],
        out_specs=[block(128, 48)] + [block(128, 256)] * 3 + [block(128, 128)],
        out_shape=[jax.ShapeDtypeStruct((rows, 128, 48), BF16)]
        + [jax.ShapeDtypeStruct((rows, 128, 256), BF16)] * 3
        + [jax.ShapeDtypeStruct((rows, 128, 128), F32)],
        scratch_shapes=[pltpu.VMEM((48, 128), BF16)] + [pltpu.VMEM((256, 256), BF16)] * 3,
        compiler_params=pltpu.CompilerParams(vmem_limit_bytes=24 * MIB),
        cost_estimate=pl.CostEstimate(flops=8 * 10**9, bytes_accessed=9 * 10**6, transcendentals=2 * 10**6),
        name="forward",
    )(x, win, w2, w3, w4, vec)


def backward_kernel(l1_ref, l2_ref, l3_ref, l4_ref, w2_ref, w3_ref, w4_ref, vec_ref,
                    corr_ref, l4t_ref, d3t_ref, d2t_ref, d1t_ref, s2, s3, s4, wt):
    @pl.when(pl.program_id(0) == 0)
    def _():
        for raw, kept in ((w2_ref, s2), (w3_ref, s3), (w4_ref, s4)):
            kept[...] = stacked(raw[...])
        wt[...] = jnp.broadcast_to(vec_ref[4:5], (128, 128)).T

    layer = l4_ref[...].reshape(GROUP * 128, 128)
    for r in range(GROUP):
        turned = l4_ref[r].T
        l4t_ref[r] = turned
        corr_ref[r] = 1.0 + jnp.sum(turned * wt[...], axis=0, keepdims=True)
    delta = vec_ref[4:5] * (1.0 - layer * layer)
    for below, weights, out in ((l3_ref, s4, d3t_ref), (l2_ref, s3, d2t_ref), (l1_ref, s2, d1t_ref)):
        layer = joined(below[...].reshape(GROUP * 128, 256))
        delta = times(pair(delta), weights[...]) * (1.0 - layer * layer)
        for r in range(GROUP):
            out[r] = delta[r * 128 : (r + 1) * 128].T


def backward_call(l1, l2, l3, l4, w2, w3, w4, vec, rows):
    whole = lambda shape: pl.BlockSpec(shape, lambda i: (0, 0))
    block = lambda a, b: pl.BlockSpec((GROUP, a, b), lambda i: (i, 0, 0))
    return pl.pallas_call(
        backward_kernel,
        grid=(rows // GROUP,),
        in_specs=[block(128, 256)] * 3 + [block(128, 128)] + [whole((128, 128))] * 3 + [whole((8, 128))],
        out_specs=[block(1, 128)] + [block(128, 128)] * 4,
        out_shape=[jax.ShapeDtypeStruct((rows, 1, 128), F32)]
        + [jax.ShapeDtypeStruct((rows, 128, 128), F32)] * 4,
        scratch_shapes=[pltpu.VMEM((256, 256), BF16)] * 3 + [pltpu.VMEM((128, 128), F32)],
        compiler_params=pltpu.CompilerParams(vmem_limit_bytes=24 * MIB),
        cost_estimate=pl.CostEstimate(flops=8 * 10**9, bytes_accessed=17 * 10**6, transcendentals=0),
        name="backward",
    )(l1, l2, l3, l4, w2, w3, w4, vec)


def pack_kernel(up_ref, inv_ref, cpl_ref, mis_ref, down_ref, right_ref, left_ref):
    rows = mis_ref.shape[1]
    tiles = rows // 8 + 2
    lane = lax.broadcasted_iota(jnp.int32, (8, 128), 1)

    def tile(a, t):
        if t == 0:
            return up_ref[a]
        if t == tiles - 1:
            return down_ref[a]
        at = pl.ds(8 * (t - 1), 8)
        if a < 36:
            return inv_ref[a, at]
        return cpl_ref[a - 36, at] if a < 40 else mis_ref[a - 40, at]

    for t in range(tiles):
        for j in range(3):
            right = jnp.zeros((8, 128), F32)
            left = jnp.zeros((8, 128), F32)
            for k in range(min(16, 46 - 16 * j)):
                value = tile(16 * j + k, t)
                here = (lane >= 8 * k) & (lane < 8 * k + 8)
                right = jnp.where(here, pltpu.roll(value, (8 * k + 8) % 128, 1), right)
                left = jnp.where(here, pltpu.roll(value, 8 * k, 1) if k else value, left)
            right_ref[j, pl.ds(8 * t, 8)] = right
            left_ref[j, pl.ds(8 * t, 8)] = left


def pack_call(up, inv, cpl, mis, down):
    rows = mis.shape[1]
    return pl.pallas_call(
        pack_kernel,
        out_shape=[jax.ShapeDtypeStruct((3, rows + 16, 128), F32)] * 2,
        name="pack",
    )(up, inv, cpl, mis, down)


def final_kernel(up_ref, inv_ref, cpl_ref, mis_ref, down_ref, prod_ref, froml_ref, fromr_ref,
                 xc_hbm, l1_hbm, l2_hbm, l3_hbm, l4t_hbm, d3t_hbm, d2t_hbm, d1t_hbm, vec_ref,
                 adj_ref, sens_ref, sums_ref,
                 ext, main, side, wt, acc4, acc3, acc2, acc1, flat,
                 xc, l1, l2, l3, l4t, d3t, d2t, d1t, sem):
    moves = [
        pltpu.make_async_copy(source, target, sem.at[i])
        for i, (source, target) in enumerate(
            ((l4t_hbm, l4t), (l3_hbm, l3), (d3t_hbm, d3t), (l2_hbm, l2),
             (d2t_hbm, d2t), (l1_hbm, l1), (d1t_hbm, d1t), (xc_hbm, xc)))
    ]
    for move in moves:
        move.start()

    rows = mis_ref.shape[1]
    tiles = rows // 8 + 2
    lane = lax.broadcasted_iota(jnp.int32, (8, 128), 1)
    first, last = lane == 0, lane == 127

    def tile(a, t):
        if t == 0:
            return up_ref[a]
        if t == tiles - 1:
            return down_ref[a]
        at = pl.ds(8 * (t - 1), 8)
        if a < 36:
            return inv_ref[a, at]
        return cpl_ref[a - 36, at] if a < 40 else mis_ref[a - 40, at]

    for a in range(46):
        j, k = a // 16, a % 16
        for t in range(tiles):
            at = pl.ds(8 * t, 8)
            high = fromr_ref[j, at]
            low = froml_ref[j, at]
            high = pltpu.roll(high, (128 - 8 * k) % 128, 1) if k else high
            low = pltpu.roll(low, 120 - 8 * k, 1) if k != 15 else low
            ext[a, at] = jnp.where(lane < 8, high, jnp.where(lane >= 120, low, 0.0))

    edge = jnp.zeros((8, 128), F32)
    for field in (main, side):
        for s in range(2):
            for i in range(6):
                field[s, i, 0:8] = edge
                field[s, i, pl.ds(8 * tiles + 8, 8)] = edge

    def solve(field, s, t, coefficient, rhs):
        for i in range(6):
            total = coefficient(6 * i) * rhs[0]
            for j in range(1, 6):
                total = total + coefficient(6 * i + j) * rhs[j]
            field[s, i, pl.ds(8 * t + 8, 8)] = total

    for t in range(tiles):
        at = pl.ds(8 * t, 8)
        solve(main, 0, t, lambda a: tile(a, t), [tile(40 + i, t) for i in range(6)])
        solve(side, 0, t, lambda a: ext[a, at], [ext[40 + i, at] for i in range(6)])

    def sweep(n, carry):
        s = lax.rem(n, 2)
        for t in range(tiles):
            at = pl.ds(8 * t, 8)
            near, beside = [], []
            for i in range(6):
                m = main[s, i, pl.ds(8 * t + 8, 8)]
                e = side[s, i, pl.ds(8 * t + 8, 8)]
                m_low, m_high = pltpu.roll(m, 1, 1), pltpu.roll(m, 127, 1)
                e_low, e_high = pltpu.roll(e, 1, 1), pltpu.roll(e, 127, 1)
                rhs = tile(40 + i, t) + tile(36, t) * main[s, i, pl.ds(8 * t + 7, 8)]
                rhs = rhs + tile(37, t) * main[s, i, pl.ds(8 * t + 9, 8)]
                rhs = rhs + tile(38, t) * jnp.where(first, e_low, m_low)
                near.append(rhs + tile(39, t) * jnp.where(last, e_high, m_high))
                rhs = ext[40 + i, at] + ext[36, at] * side[s, i, pl.ds(8 * t + 7, 8)]
                rhs = rhs + ext[37, at] * side[s, i, pl.ds(8 * t + 9, 8)]
                rhs = rhs + ext[38, at] * jnp.where(first, m_low, e_low)
                beside.append(rhs + ext[39, at] * jnp.where(last, m_high, e_high))
            solve(main, 1 - s, t, lambda a: tile(a, t), near)
            solve(side, 1 - s, t, lambda a: ext[a, at], beside)
        return carry

    lax.fori_loop(0, SWEEPS - 1, sweep, 0)
    done = (SWEEPS - 1) % 2

    square = jnp.zeros((8, 128), F32)
    for t in range(rows // 8):
        at = pl.ds(8 * t, 8)
        total = jnp.zeros((8, 128), F32)
        for i in range(6):
            value = main[done, i, pl.ds(8 * t + 16, 8)]
            adj_ref[i, at] = value
            total = total + value * prod_ref[i, at]
        sens_ref[at] = -total
        square = square + total * total

    wt[...] = jnp.broadcast_to(vec_ref[4:5], (128, 128)).T
    for acc in (acc4, acc3, acc2, acc1):
        acc[...] = jnp.zeros_like(acc)
    flat[...] = jnp.zeros_like(flat)

    def term(scaled, layer, acc, slot, g):
        total = flat[slot]
        pieces = []
        for value in scaled:
            total = total + value
            high, low = split(value)
            pieces.append(jnp.concatenate([high, low], axis=0))
        flat[slot] = total
        left = jnp.concatenate(pieces, axis=1)
        right = layer[pl.ds(2 * g, 2)].reshape(256, layer.shape[2])
        acc[...] += jnp.dot(left, right, preferred_element_type=F32)

    def both(g):
        return [sens_ref[pl.ds(2 * g + r, 1), :] for r in range(2)]

    for move in moves[:2]:
        move.wait()

    def top(g, carry):
        weights = both(g)
        out = flat[4]
        scaled = []
        for r in range(2):
            value = l4t[2 * g + r]
            out = out + value * weights[r]
            scaled.append(wt[...] * (1.0 - value * value) * weights[r])
        flat[4] = out
        term(scaled, l3, acc4, 3, g)
        return carry

    lax.fori_loop(0, rows // 2, top, 0)

    for n, (delta, layer, acc, slot) in enumerate(((d3t, l2, acc3, 2), (d2t, l1, acc2, 1), (d1t, xc, acc1, 0))):
        for move in moves[2 + 2 * n : 4 + 2 * n]:
            move.wait()

        def lower(g, carry):
            weights = both(g)
            term([delta[2 * g + r] * weights[r] for r in range(2)], layer, acc, slot, g)
            return carry

        lax.fori_loop(0, rows // 2, lower, 0)

    for n, acc in enumerate((acc4, acc3, acc2)):
        sums_ref[pl.ds(128 * n, 128)] = (acc[0:128, 0:128] + acc[128:256, 0:128]) + (
            acc[0:128, 128:256] + acc[128:256, 128:256])
    lanes = lax.broadcasted_iota(jnp.int32, (128, 128), 1)
    block = jnp.zeros((128, 128), F32)
    for slot in range(5):
        block = jnp.where(lanes == 16 + slot, jnp.sum(flat[slot], axis=1, keepdims=True), block)
    block = jnp.where(lanes == 21, jnp.sum(square), block)
    own = acc1[0:128] + acc1[128:256]
    own = jnp.concatenate([own, jnp.zeros((128, 80), F32)], axis=1)
    own = own + pltpu.roll(own, 112, 1)
    sums_ref[pl.ds(384, 128)] = jnp.where(lanes < 12, own, block)


def final_call(up, inv, cpl, mis, down, prod, froml, fromr, xc, l1, l2, l3, l4t, d3t, d2t, d1t, vec):
    rows = mis.shape[1]
    vmem = pl.BlockSpec(memory_space=pltpu.VMEM)
    hbm = pl.BlockSpec(memory_space=pl.ANY)
    big = [l1, l2, l3, l4t, d3t, d2t, d1t]
    return pl.pallas_call(
        final_kernel,
        in_specs=[vmem] * 8 + [hbm] * 8 + [vmem],
        out_specs=[vmem] * 3,
        out_shape=[
            jax.ShapeDtypeStruct((6, rows, 128), F32),
            jax.ShapeDtypeStruct((rows, 128), F32),
            jax.ShapeDtypeStruct((512, 128), F32),
        ],
        scratch_shapes=[
            pltpu.VMEM((46, rows + 16, 128), F32),
            pltpu.VMEM((2, 6, rows + 32, 128), F32),
            pltpu.VMEM((2, 6, rows + 32, 128), F32),
            pltpu.VMEM((128, 128), F32),
            pltpu.VMEM((256, 256), F32),
            pltpu.VMEM((256, 256), F32),
            pltpu.VMEM((256, 256), F32),
            pltpu.VMEM((256, 48), F32),
            pltpu.VMEM((5, 128, 128), F32),
            pltpu.VMEM(xc.shape, BF16),
        ]
        + [pltpu.VMEM(value.shape, value.dtype) for value in big]
        + [pltpu.SemaphoreType.DMA((8,))],
        compiler_params=pltpu.CompilerParams(vmem_limit_bytes=40 * MIB),
        name="final",
    )(up, inv, cpl, mis, down, prod, froml, fromr, xc, *big, vec)


def unpack_kernel(sums_ref, w4_ref, w3_ref, w2_ref, win_ref, b1_ref, b2_ref, b3_ref, b4_ref, out_ref):
    block = sums_ref[pl.ds(384, 128)]
    scale = 1.0 / jnp.sqrt(jnp.broadcast_to(block[0:1, 21:22], (1, 128)) + EPS)
    for n, ref in enumerate((w4_ref, w3_ref, w2_ref)):
        ref[...] = sums_ref[pl.ds(128 * n, 128)] * scale
    block = block * scale
    win_ref[...] = block[:, 0:12]
    turned = block.T
    for n, ref in enumerate((b1_ref, b2_ref, b3_ref, b4_ref, out_ref)):
        ref[...] = turned[16 + n : 17 + n]


def unpack_call(sums):
    shapes = [(128, 128)] * 3 + [(128, 12)] + [(1, 128)] * 5
    return pl.pallas_call(
        unpack_kernel,
        out_shape=[jax.ShapeDtypeStruct(shape, F32) for shape in shapes],
        name="unpack",
    )(sums)


def shifted(last, initial, axes, wrap):
    size = lax.axis_size(axes)
    up = [(i, (i + 1) % size) for i in range(size if wrap else size - 1)]
    down = [(j, i) for i, j in up]
    return lax.ppermute(last, axes, up), lax.ppermute(initial, axes, down)


def summed(value):
    near, far = lax.axis_size(NEAR), lax.axis_size(FAR)
    rows = value.shape[0] // near
    part = lax.all_to_all(value.reshape(near, rows, 128), NEAR, 0, 0)
    part = jnp.sum(part, axis=0)
    part = lax.all_to_all(jnp.broadcast_to(part[None], (far, rows, 128)), FAR, 0, 0)
    part = jnp.sum(part, axis=0)
    whole = lax.all_to_all(jnp.broadcast_to(part[None], (near, rows, 128)), NEAR, 0, 0)
    return whole.reshape(near * rows, 128)


def local(features, inverse_diag, couplings, mismatch, production, weight_in, bias_in, weight_two,
          bias_two, weight_three, bias_three, weight_four, bias_four, weight_out):
    nvars, rows, cols = mismatch.shape
    inverse = inverse_diag.reshape(nvars * nvars, rows, cols)
    fields = (inverse, couplings, mismatch)
    last = jnp.concatenate([field[:, rows - 8 :] for field in fields], axis=0)
    initial = jnp.concatenate([field[:, :8] for field in fields], axis=0)
    above, below = shifted(last, initial, SUB, False)

    x = jnp.pad(jnp.transpose(features, (1, 0, 2)), ((0, 0), (0, 4), (0, 0)))
    win = jnp.pad(weight_in.T, ((0, 4), (0, 0)))
    vec = jnp.stack([bias_in, bias_two, bias_three, bias_four] + [weight_out] * 4)
    xc, l1, l2, l3, l4 = forward_call(x, win, weight_two, weight_three, weight_four, vec, rows)

    right, left = pack_call(above, inverse, couplings, mismatch, below)
    from_low, from_high = shifted(right, left, BLK, True)
    correction, l4t, d3t, d2t, d1t = backward_call(
        l1, l2, l3, l4, weight_two, weight_three, weight_four, vec, rows)

    adjoint, sensitivity, sums = final_call(
        above, inverse, couplings, mismatch, below, production, from_low, from_high,
        xc, l1, l2, l3, l4t, d3t, d2t, d1t, vec)
    g4, g3, g2, gin, b1, b2, b3, b4, gout = unpack_call(summed(sums))
    flat = lambda value: value.reshape(128)
    return (adjoint, sensitivity, correction.reshape(rows, cols), gin, flat(b1), g2, flat(b2),
            g3, flat(b3), g4, flat(b4), flat(gout))


def solution(mesh):
    sizes = (16, 2, 2, 4, 2) if mesh.devices.size == 512 else (mesh.shape["blk"], 1, 1, mesh.shape["sub"], 1)
    fine = Mesh(mesh.devices.reshape(sizes), BLK + SUB)
    three = P(None, SUB, BLK)
    two = P(SUB, BLK)
    return jax.shard_map(
        local,
        mesh=fine,
        in_specs=(three, P(None, None, SUB, BLK), three, three, three) + (P(),) * 9,
        out_specs=(three, two, two) + (P(),) * 9,
        check_vma=False,
    )
```

```python
import functools
import jax
import jax.numpy as jnp
from jax import lax
from jax.experimental import pallas as pl
from jax.experimental.pallas import tpu as pltpu
from jax.sharding import Mesh, PartitionSpec as P

SWEEPS = 8
EPS = 1e-06
BLK = ("z", "xh", "c")
SUB = ("y", "xl")
NEAR = ("xh", "c", "y", "xl")
FAR = ("z",)
F32 = jnp.float32
BF16 = jnp.bfloat16
GROUP = 4
WIDE = 4
PARTS = 4
MIB = 1 << 20
LIMIT = 8 * MIB


def split(value):
    high = value.astype(BF16)
    return high, (value - high.astype(F32)).astype(BF16)


def pair(value):
    return jnp.concatenate(split(value), axis=1)


def joined(both):
    return both[:, :128].astype(F32) + both[:, 128:].astype(F32)


def times(both, weights):
    out = jnp.dot(both, weights, preferred_element_type=F32)
    return out[:, :128] + out[:, 128:]


def stacked(weight):
    both = pair(weight)
    return jnp.concatenate([both, both], axis=0)


VMEM = pl.BlockSpec(memory_space=pltpu.VMEM)
ANY = pl.BlockSpec(memory_space=pl.ANY)
HBM = pl.BlockSpec(memory_space=pltpu.MemorySpace.HBM)


def network_rows(x_ref, base, count, prepared, vectors, outs):
    s1, f2, f3, f4, b2, b3, b4, wt = prepared
    bias1, bias2, bias3, bias4, wout = (vectors.at[pl.ds(n, 1)] for n in range(5))
    corr_ref, xc_ref, l1_ref, l2_ref, l3_ref, l4t_ref, d3t_ref, d2t_ref, d1t_ref = outs
    pad = jnp.zeros((4, 128), F32)

    def step(g, carry):
        at = GROUP * g
        columns = []
        for r in range(GROUP):
            x = jnp.concatenate([x_ref[:, base + at + r, :], pad], axis=0)
            high = x.astype(BF16).astype(F32)
            column = jnp.concatenate([high, x - high, high], axis=0).T.astype(BF16)
            xc_ref[at + r] = column
            columns.append(column)
        inputs = jnp.concatenate(columns, axis=0)
        layer = jnp.tanh(jnp.dot(inputs, s1[...], preferred_element_type=F32) + bias1[...])
        layers = []
        for out, weights, bias in ((l1_ref, f2, bias2), (l2_ref, f3, bias3), (l3_ref, f4, bias4)):
            layers.append(layer)
            both = pair(layer)
            out[pl.ds(at, GROUP)] = both.reshape(GROUP, 128, 256)
            layer = jnp.tanh(times(both, weights[...]) + bias[...])
        for r in range(GROUP):
            turned = layer[128 * r : 128 * r + 128].T
            l4t_ref[at + r] = turned
            corr_ref[at + r] = 1.0 + jnp.sum(turned * wt[...], axis=0, keepdims=True)
        delta = wout[...] * (1.0 - layer * layer)
        for weights, out in ((b4, d3t_ref), (b3, d2t_ref), (b2, d1t_ref)):
            layer = layers.pop()
            delta = times(pair(delta), weights[...]) * (1.0 - layer * layer)
            for r in range(GROUP):
                out[at + r] = delta[128 * r : 128 * r + 128].T
        return carry

    lax.fori_loop(0, count // GROUP, step, 0)


def network_shapes(count):
    return [
        jax.ShapeDtypeStruct((count, 1, 128), F32),
        jax.ShapeDtypeStruct((count, 128, 48), BF16),
    ] + [jax.ShapeDtypeStruct((count, 128, 256), BF16)] * 3 + [jax.ShapeDtypeStruct((count, 128, 128), F32)] * 4


PREPARED = [jax.ShapeDtypeStruct((48, 128), BF16)] + [jax.ShapeDtypeStruct((256, 256), BF16)] * 6 + [
    jax.ShapeDtypeStruct((128, 128), F32)]


def cost(count):
    return pl.CostEstimate(flops=count * 3 * 10**8, bytes_accessed=count * 1000, transcendentals=0)


def strips(fields, out, row, sem):
    moves, at = [], 0
    for i, field in enumerate(fields):
        n = field.shape[0]
        moves.append(pltpu.make_async_copy(field.at[:, pl.ds(row, 8)], out.at[pl.ds(at, n)], sem.at[i]))
        at += n
    for move in moves:
        move.start()
    return moves


def last_kernel(inv_hbm, cpl_hbm, mis_hbm, out_hbm, sem):
    rows = mis_hbm.shape[1]
    for move in strips((inv_hbm, cpl_hbm, mis_hbm), out_hbm, rows - 8, sem):
        move.wait()


def last_call(inv, cpl, mis):
    return pl.pallas_call(
        last_kernel,
        in_specs=[HBM] * 3,
        out_specs=ANY,
        out_shape=jax.ShapeDtypeStruct((46, 8, 128), F32),
        scratch_shapes=[pltpu.SemaphoreType.DMA((3,))],
        compiler_params=pltpu.CompilerParams(vmem_limit_bytes=MIB),
        name="last_rows",
    )(inv, cpl, mis)


def opening_kernel(base, count, last_hbm, inv_hbm, cpl_hbm, mis_hbm, x_hbm, win_hbm, w2_hbm, w3_hbm, w4_hbm, *rest):
    vectors, rest = rest[:5], rest[5:]
    strip, x_ref, vec, prepared, outs = rest[0], rest[1], rest[2], rest[3:11], rest[11:20]
    win_ref, w2_ref, w3_ref, w4_ref, sem, strip_sem = rest[20:]
    moves = [
        pltpu.make_async_copy(source, target, sem.at[i])
        for i, (source, target) in enumerate(
            [(w2_hbm, w2_ref), (w3_hbm, w3_ref), (w4_hbm, w4_ref), (win_hbm, win_ref), (x_hbm, x_ref)]
            + [(vector, vec.at[pl.ds(n, 1)]) for n, vector in enumerate(vectors)])
    ]
    for move in moves:
        move.start()
    held = strips((inv_hbm, cpl_hbm, mis_hbm), strip, 0, strip_sem)
    s1, f2, f3, f4, b2, b3, b4, wt = prepared
    for move in moves:
        move.wait()
    win = jnp.concatenate([win_ref[...], jnp.zeros((4, 128), F32)], axis=0)
    high = win.astype(BF16).astype(F32)
    s1[...] = jnp.concatenate([high, high, win - high], axis=0).astype(BF16)
    for raw, ahead, back in ((w2_ref, f2, b2), (w3_ref, f3, b3), (w4_ref, f4, b4)):
        ahead[...] = stacked(raw[...].T)
        back[...] = stacked(raw[...])
    wt[...] = jnp.broadcast_to(vec[4:5], (128, 128)).T
    network_rows(x_ref, base, count, prepared, vec, outs)
    for move in held:
        move.wait()


def opening_call(base, count, last, inv, cpl, mis, x, win, w2, w3, w4, vectors):
    return pl.pallas_call(
        functools.partial(opening_kernel, base, count),
        in_specs=[ANY] + [HBM] * 13,
        out_specs=[ANY] + [VMEM] * 19,
        out_shape=[jax.ShapeDtypeStruct((46, 8, 128), F32), jax.ShapeDtypeStruct(x.shape, F32),
                   jax.ShapeDtypeStruct((8, 128), F32)] + PREPARED + network_shapes(count),
        scratch_shapes=[pltpu.VMEM((12, 128), F32)] + [pltpu.VMEM((128, 128), F32)] * 3
        + [pltpu.SemaphoreType.DMA((10,)), pltpu.SemaphoreType.DMA((3,))],
        compiler_params=pltpu.CompilerParams(vmem_limit_bytes=LIMIT),
        cost_estimate=cost(count),
        name="network_first",
    )(last, inv, cpl, mis, x, win, w2, w3, w4, *vectors)


def middle_kernel(base, count, token, x_ref, *rest):
    network_rows(x_ref, base, count, rest[:8], rest[8], rest[9:])


def middle_call(base, count, token, x, prepared, vectors):
    return pl.pallas_call(
        functools.partial(middle_kernel, base, count),
        in_specs=[ANY] + [VMEM] * 10,
        out_specs=[VMEM] * 9,
        out_shape=network_shapes(count),
        compiler_params=pltpu.CompilerParams(vmem_limit_bytes=LIMIT),
        cost_estimate=cost(count),
        name="network",
    )(token, x, *prepared, vectors)


def packed(up_ref, inv_ref, cpl_ref, mis_ref, down_ref, out_ref, offset):
    rows = mis_ref.shape[1]
    tiles = rows // 8 + 2
    lane = lax.broadcasted_iota(jnp.int32, (8, 128), 1)
    for t in range(tiles):
        for j in range(3):
            out = jnp.zeros((8, 128), F32)
            for k in range(min(16, 46 - 16 * j)):
                value = tile_of(up_ref, inv_ref, cpl_ref, mis_ref, down_ref, 16 * j + k, t)
                by = (8 * k - offset) % 128
                here = (lane >= 8 * k) & (lane < 8 * k + 8)
                out = jnp.where(here, pltpu.roll(value, by, 1) if by else value, out)
            out_ref[j, pl.ds(8 * t, 8)] = out


def tile_of(up_ref, inv_ref, cpl_ref, mis_ref, down_ref, a, t):
    if t == 0:
        return up_ref[a]
    if t == mis_ref.shape[1] // 8 + 1:
        return down_ref[a]
    at = pl.ds(8 * (t - 1), 8)
    if a < 36:
        return inv_ref[a, at]
    return cpl_ref[a - 36, at] if a < 40 else mis_ref[a - 40, at]


def right_kernel(up_ref, inv_ref, cpl_ref, mis_ref, down_ref, out_ref):
    packed(up_ref, inv_ref, cpl_ref, mis_ref, down_ref, out_ref, 120)


def right_call(up, inv, cpl, mis, down):
    rows = mis.shape[1]
    return pl.pallas_call(
        right_kernel,
        in_specs=[VMEM] * 5,
        out_specs=VMEM,
        out_shape=jax.ShapeDtypeStruct((3, rows + 16, 128), F32),
        compiler_params=pltpu.CompilerParams(vmem_limit_bytes=LIMIT),
        name="right_columns",
    )(up, inv, cpl, mis, down)


def third_kernel(base, count, up_ref, inv_ref, cpl_ref, mis_ref, down_ref, x_ref, *rest):
    network_rows(x_ref, base, count, rest[:8], rest[8], rest[10:])
    packed(up_ref, inv_ref, cpl_ref, mis_ref, down_ref, rest[9], 0)


def third_call(base, count, up, inv, cpl, mis, down, x, prepared, vectors):
    rows = mis.shape[1]
    return pl.pallas_call(
        functools.partial(third_kernel, base, count),
        in_specs=[VMEM] * 15,
        out_specs=[VMEM] * 10,
        out_shape=[jax.ShapeDtypeStruct((3, rows + 16, 128), F32)] + network_shapes(count),
        compiler_params=pltpu.CompilerParams(vmem_limit_bytes=LIMIT),
        cost_estimate=cost(count),
        name="network_left",
    )(up, inv, cpl, mis, down, x, *prepared, vectors)


def final_kernel(up_ref, inv_ref, cpl_ref, mis_ref, down_ref, prod_ref, froml_ref, fromr_ref, wt, *rest):
    parts = [rest[8 * p : 8 * p + 8] for p in range(PARTS)]
    adj_ref, sens_ref, sums_ref, ext, main, side, acc4, acc3, acc2, acc1, flat = rest[8 * PARTS :]
    rows = mis_ref.shape[1]
    tiles = rows // 8 + 2
    lane = lax.broadcasted_iota(jnp.int32, (8, 128), 1)
    first, last = lane == 0, lane == 127

    def tile(a, t):
        return tile_of(up_ref, inv_ref, cpl_ref, mis_ref, down_ref, a, t)

    for a in range(46):
        j, k = a // 16, a % 16
        for t in range(tiles):
            at = pl.ds(8 * t, 8)
            high = fromr_ref[j, at]
            low = froml_ref[j, at]
            high = pltpu.roll(high, (128 - 8 * k) % 128, 1) if k else high
            low = pltpu.roll(low, 120 - 8 * k, 1) if k != 15 else low
            ext[a, at] = jnp.where(lane < 8, high, jnp.where(lane >= 120, low, 0.0))

    edge = jnp.zeros((8, 128), F32)
    for field in (main, side):
        for s in range(2):
            for i in range(6):
                field[s, i, 0:8] = edge
                field[s, i, pl.ds(8 * tiles + 8, 8)] = edge

    def solve(field, s, t, coefficient, rhs):
        for i in range(6):
            total = coefficient(6 * i) * rhs[0]
            for j in range(1, 6):
                total = total + coefficient(6 * i + j) * rhs[j]
            field[s, i, pl.ds(8 * t + 8, 8)] = total

    for t in range(tiles):
        at = pl.ds(8 * t, 8)
        solve(main, 0, t, lambda a: tile(a, t), [tile(40 + i, t) for i in range(6)])
        solve(side, 0, t, lambda a: ext[a, at], [ext[40 + i, at] for i in range(6)])

    def sweep(n, carry):
        s = lax.rem(n, 2)
        for t in range(tiles):
            at = pl.ds(8 * t, 8)
            near, beside = [], []
            for i in range(6):
                m = main[s, i, pl.ds(8 * t + 8, 8)]
                e = side[s, i, pl.ds(8 * t + 8, 8)]
                m_low, m_high = pltpu.roll(m, 1, 1), pltpu.roll(m, 127, 1)
                e_low, e_high = pltpu.roll(e, 1, 1), pltpu.roll(e, 127, 1)
                rhs = tile(40 + i, t) + tile(36, t) * main[s, i, pl.ds(8 * t + 7, 8)]
                rhs = rhs + tile(37, t) * main[s, i, pl.ds(8 * t + 9, 8)]
                rhs = rhs + tile(38, t) * jnp.where(first, e_low, m_low)
                near.append(rhs + tile(39, t) * jnp.where(last, e_high, m_high))
                rhs = ext[40 + i, at] + ext[36, at] * side[s, i, pl.ds(8 * t + 7, 8)]
                rhs = rhs + ext[37, at] * side[s, i, pl.ds(8 * t + 9, 8)]
                rhs = rhs + ext[38, at] * jnp.where(first, m_low, e_low)
                beside.append(rhs + ext[39, at] * jnp.where(last, m_high, e_high))
            solve(main, 1 - s, t, lambda a: tile(a, t), near)
            solve(side, 1 - s, t, lambda a: ext[a, at], beside)
        return carry

    lax.fori_loop(0, SWEEPS - 1, sweep, 0)
    done = (SWEEPS - 1) % 2

    square = jnp.zeros((8, 128), F32)
    for t in range(rows // 8):
        at = pl.ds(8 * t, 8)
        total = jnp.zeros((8, 128), F32)
        for i in range(6):
            value = main[done, i, pl.ds(8 * t + 16, 8)]
            adj_ref[i, at] = value
            total = total + value * prod_ref[i, at]
        sens_ref[at] = -total
        square = square + total * total

    for acc in (acc4, acc3, acc2, acc1):
        acc[...] = jnp.zeros_like(acc)
    flat[...] = jnp.zeros_like(flat)

    def term(scaled, right, acc, slot):
        total = flat[slot]
        pieces = []
        for value in scaled:
            total = total + value
            high, low = split(value)
            pieces.append(jnp.concatenate([high, low], axis=0))
        flat[slot] = total
        left = jnp.concatenate(pieces, axis=1)
        acc[...] += jnp.dot(left, right.reshape(128 * len(pieces), right.shape[2]), preferred_element_type=F32)

    base = 0
    for part in parts:
        xc, l1, l2, l3, l4t, d3t, d2t, d1t = part

        def gather(g, carry, base=base, part=part):
            xc, l1, l2, l3, l4t, d3t, d2t, d1t = part
            at = WIDE * g
            some = pl.ds(at, WIDE)
            weights = [sens_ref[pl.ds(base + at + r, 1), :] for r in range(WIDE)]
            out = flat[4]
            scaled = []
            for r in range(WIDE):
                value = l4t[at + r]
                out = out + value * weights[r]
                scaled.append(wt[...] * (1.0 - value * value) * weights[r])
            flat[4] = out
            term(scaled, l3[some], acc4, 3)
            for delta, layer, acc, slot in ((d3t, l2, acc3, 2), (d2t, l1, acc2, 1), (d1t, xc, acc1, 0)):
                term([delta[at + r] * weights[r] for r in range(WIDE)], layer[some], acc, slot)
            return carry

        lax.fori_loop(0, l1.shape[0] // WIDE, gather, 0)
        base += l1.shape[0]

    for n, acc in enumerate((acc4, acc3, acc2)):
        sums_ref[pl.ds(128 * n, 128)] = (acc[0:128, 0:128] + acc[128:256, 0:128]) + (
            acc[0:128, 128:256] + acc[128:256, 128:256])
    lanes = lax.broadcasted_iota(jnp.int32, (128, 128), 1)
    block = jnp.zeros((128, 128), F32)
    for slot in range(5):
        block = jnp.where(lanes == 16 + slot, jnp.sum(flat[slot], axis=1, keepdims=True), block)
    block = jnp.where(lanes == 21, jnp.sum(square), block)
    own = acc1[0:128] + acc1[128:256]
    own = jnp.concatenate([own, jnp.zeros((128, 80), F32)], axis=1)
    own = own + pltpu.roll(own, 112, 1)
    sums_ref[pl.ds(384, 128)] = jnp.where(lanes < 12, own, block)


def final_call(up, inv, cpl, mis, down, prod, froml, fromr, wt, parts):
    rows = mis.shape[1]
    flat = [value for part in parts for value in part]
    return pl.pallas_call(
        final_kernel,
        in_specs=[VMEM] * (9 + len(flat)),
        out_specs=[VMEM] * 3,
        out_shape=[
            jax.ShapeDtypeStruct((6, rows, 128), F32),
            jax.ShapeDtypeStruct((rows, 128), F32),
            jax.ShapeDtypeStruct((512, 128), F32),
        ],
        scratch_shapes=[
            pltpu.VMEM((46, rows + 16, 128), F32),
            pltpu.VMEM((2, 6, rows + 32, 128), F32),
            pltpu.VMEM((2, 6, rows + 32, 128), F32),
            pltpu.VMEM((256, 256), F32),
            pltpu.VMEM((256, 256), F32),
            pltpu.VMEM((256, 256), F32),
            pltpu.VMEM((256, 48), F32),
            pltpu.VMEM((5, 128, 128), F32),
        ],
        compiler_params=pltpu.CompilerParams(vmem_limit_bytes=LIMIT),
        name="final",
    )(up, inv, cpl, mis, down, prod, froml, fromr, wt, *flat)


def unpack_kernel(sums_ref, w4_ref, w3_ref, w2_ref, win_ref, b1_ref, b2_ref, b3_ref, b4_ref, out_ref):
    block = sums_ref[pl.ds(384, 128)]
    scale = 1.0 / jnp.sqrt(jnp.broadcast_to(block[0:1, 21:22], (1, 128)) + EPS)
    for n, ref in enumerate((w4_ref, w3_ref, w2_ref)):
        ref[...] = sums_ref[pl.ds(128 * n, 128)] * scale
    block = block * scale
    turned = block.T
    win_ref[...] = turned[0:12]
    for n, ref in enumerate((b1_ref, b2_ref, b3_ref, b4_ref, out_ref)):
        ref[...] = turned[16 + n : 17 + n]


def unpack_call(sums):
    shapes = [(128, 128)] * 3 + [(12, 128)] + [(1, 128)] * 5
    return pl.pallas_call(
        unpack_kernel,
        in_specs=[VMEM],
        out_shape=[jax.ShapeDtypeStruct(shape, F32) for shape in shapes],
        name="unpack",
    )(sums)


def sent(value, axes, wrap, by):
    size = lax.axis_size(axes)
    pairs = [(i, (i + by) % size) for i in range(size) if wrap or 0 <= i + by < size]
    return lax.ppermute(value, axes, pairs)


def summed(value):
    near, far = lax.axis_size(NEAR), lax.axis_size(FAR)
    rows = value.shape[0] // near
    part = lax.all_to_all(value.reshape(near, rows, 128), NEAR, 0, 0)
    part = jnp.sum(part, axis=0)
    part = lax.all_to_all(jnp.broadcast_to(part[None], (far, rows, 128)), FAR, 0, 0)
    part = jnp.sum(part, axis=0)
    whole = lax.all_to_all(jnp.broadcast_to(part[None], (near, rows, 128)), NEAR, 0, 0)
    return whole.reshape(near * rows, 128)


def local(features, inverse_diag, couplings, mismatch, production, weight_in, bias_in, weight_two,
          bias_two, weight_three, bias_three, weight_four, bias_four, weight_out):
    nvars, rows, cols = mismatch.shape
    inverse = inverse_diag.reshape(nvars * nvars, rows, cols)
    win = weight_in.T
    vectors = [v.reshape(1, 128) for v in (bias_in, bias_two, bias_three, bias_four, weight_out)]
    count = rows // PARTS

    last = last_call(inverse, couplings, mismatch)
    above = sent(last, SUB, False, 1)
    initial, features, vectors, *rest = opening_call(
        0, count, last, inverse, couplings, mismatch, features, win, weight_two, weight_three, weight_four, vectors)
    prepared, first = rest[:8], rest[8:]
    below = sent(initial, SUB, False, -1)
    second = middle_call(count, count, above, features, prepared, vectors)

    right = right_call(above, inverse, couplings, mismatch, below)
    from_low = sent(right, BLK, True, 1)
    left, *third = third_call(2 * count, count, above, inverse, couplings, mismatch, below, features,
                              prepared, vectors)
    from_high = sent(left, BLK, True, -1)
    fourth = middle_call(3 * count, count, from_low, features, prepared, vectors)

    parts = (first, second, third, fourth)
    correction = jnp.concatenate([part[0] for part in parts], axis=0)
    adjoint, sensitivity, sums = final_call(
        above, inverse, couplings, mismatch, below, production, from_low, from_high, prepared[7],
        [part[1:] for part in parts])
    g4, g3, g2, gin, b1, b2, b3, b4, gout = unpack_call(summed(sums))
    flat = lambda value: value.reshape(128)
    return (adjoint, sensitivity, correction.reshape(rows, cols), gin.T, flat(b1), g2, flat(b2),
            g3, flat(b3), g4, flat(b4), flat(gout))


def solution(mesh):
    sizes = (16, 2, 2, 4, 2) if mesh.devices.size == 512 else (mesh.shape["blk"], 1, 1, mesh.shape["sub"], 1)
    fine = Mesh(mesh.devices.reshape(sizes), BLK + SUB)
    three = P(None, SUB, BLK)
    two = P(SUB, BLK)
    return jax.shard_map(
        local,
        mesh=fine,
        in_specs=(three, P(None, None, SUB, BLK), three, three, three) + (P(),) * 9,
        out_specs=(three, two, two) + (P(),) * 9,
        check_vma=False,
    )
```

```python
import functools
import jax
import jax.numpy as jnp
from jax import lax
from jax.experimental import pallas as pl
from jax.experimental.pallas import tpu as pltpu
from jax.sharding import Mesh, PartitionSpec as P

SWEEPS = 8
EPS = 1e-06
BLK = ("z", "xh", "c")
SUB = ("y", "xl")
NEAR = ("xh", "c", "y", "xl")
FAR = ("z",)
F32 = jnp.float32
BF16 = jnp.bfloat16
GROUP = 4
WIDE = 4
PARTS = 4
MIB = 1 << 20
LIMIT = 8 * MIB


def split(value):
    high = value.astype(BF16)
    return high, (value - high.astype(F32)).astype(BF16)


def pair(value):
    return jnp.concatenate(split(value), axis=1)


def joined(both):
    return both[:, :128].astype(F32) + both[:, 128:].astype(F32)


def times(both, weights):
    out = jnp.dot(both, weights, preferred_element_type=F32)
    return out[:, :128] + out[:, 128:]


def stacked(weight):
    both = pair(weight)
    return jnp.concatenate([both, both], axis=0)


VMEM = pl.BlockSpec(memory_space=pltpu.VMEM)
ANY = pl.BlockSpec(memory_space=pl.ANY)
HBM = pl.BlockSpec(memory_space=pltpu.MemorySpace.HBM)


def network_rows(x_ref, base, count, prepared, vectors, outs):
    s1, f2, f3, f4, b2, b3, b4, wt = prepared
    bias1, bias2, bias3, bias4, wout = (vectors.at[pl.ds(n, 1)] for n in range(5))
    corr_ref, xc_ref, l1_ref, l2_ref, l3_ref, l4t_ref, d3t_ref, d2t_ref, d1t_ref = outs
    pad = jnp.zeros((4, 128), F32)

    def step(g, carry):
        at = GROUP * g
        columns = []
        for r in range(GROUP):
            x = jnp.concatenate([x_ref[:, base + at + r, :], pad], axis=0)
            high = x.astype(BF16).astype(F32)
            column = jnp.concatenate([high, x - high, high], axis=0).T.astype(BF16)
            xc_ref[at + r] = column
            columns.append(column)
        inputs = jnp.concatenate(columns, axis=0)
        layer = jnp.tanh(jnp.dot(inputs, s1[...], preferred_element_type=F32) + bias1[...])
        layers = []
        for out, weights, bias in ((l1_ref, f2, bias2), (l2_ref, f3, bias3), (l3_ref, f4, bias4)):
            layers.append(layer)
            both = pair(layer)
            out[pl.ds(at, GROUP)] = both.reshape(GROUP, 128, 256)
            layer = jnp.tanh(times(both, weights[...]) + bias[...])
        for r in range(GROUP):
            turned = layer[128 * r : 128 * r + 128].T
            l4t_ref[at + r] = turned
            corr_ref[at + r] = 1.0 + jnp.sum(turned * wt[...], axis=0, keepdims=True)
        delta = wout[...] * (1.0 - layer * layer)
        for weights, out in ((b4, d3t_ref), (b3, d2t_ref), (b2, d1t_ref)):
            layer = layers.pop()
            delta = times(pair(delta), weights[...]) * (1.0 - layer * layer)
            for r in range(GROUP):
                out[at + r] = delta[128 * r : 128 * r + 128].T
        return carry

    lax.fori_loop(0, count // GROUP, step, 0)


def network_shapes(count):
    return [
        jax.ShapeDtypeStruct((count, 1, 128), F32),
        jax.ShapeDtypeStruct((count, 128, 48), BF16),
    ] + [jax.ShapeDtypeStruct((count, 128, 256), BF16)] * 3 + [jax.ShapeDtypeStruct((count, 128, 128), F32)] * 4


PREPARED = [jax.ShapeDtypeStruct((48, 128), BF16)] + [jax.ShapeDtypeStruct((256, 256), BF16)] * 6 + [
    jax.ShapeDtypeStruct((128, 128), F32)]


def cost(count):
    return pl.CostEstimate(flops=count * 3 * 10**8, bytes_accessed=count * 1000, transcendentals=0)


def strips(fields, out, row, sem):
    moves, at = [], 0
    for i, field in enumerate(fields):
        n = field.shape[0]
        moves.append(pltpu.make_async_copy(field.at[:, pl.ds(row, 8)], out.at[pl.ds(at, n)], sem.at[i]))
        at += n
    for move in moves:
        move.start()
    return moves


def pinned(*values):
    return [pltpu.with_memory_space_constraint(value, pltpu.MemorySpace.HBM) for value in values]


def edge_kernel(inv_hbm, cpl_hbm, mis_hbm, last, initial, sem):
    rows = mis_hbm.shape[1]
    fields = (inv_hbm, cpl_hbm, mis_hbm)
    moves = strips(fields, last, rows - 8, sem.at[0]) + strips(fields, initial, 0, sem.at[1])
    for move in moves:
        move.wait()


def edge_call(inv, cpl, mis):
    return pl.pallas_call(
        edge_kernel,
        in_specs=[HBM] * 3,
        out_specs=[ANY] * 2,
        out_shape=[jax.ShapeDtypeStruct((46, 8, 128), F32)] * 2,
        scratch_shapes=[pltpu.SemaphoreType.DMA((2, 3))],
        compiler_params=pltpu.CompilerParams(vmem_limit_bytes=MIB),
        name="edge_rows",
    )(*pinned(inv, cpl, mis))


def opening_kernel(base, count, last_hbm, first_hbm, x_hbm, win_hbm, w2_hbm, w3_hbm, w4_hbm, *rest):
    vectors, rest = rest[:5], rest[5:]
    x_ref, vec, prepared, outs = rest[0], rest[1], rest[2:10], rest[10:19]
    win_ref, w2_ref, w3_ref, w4_ref, sem = rest[19:]
    moves = [
        pltpu.make_async_copy(source, target, sem.at[i])
        for i, (source, target) in enumerate(
            [(w2_hbm, w2_ref), (w3_hbm, w3_ref), (w4_hbm, w4_ref), (win_hbm, win_ref), (x_hbm, x_ref)]
            + [(vector, vec.at[pl.ds(n, 1)]) for n, vector in enumerate(vectors)])
    ]
    for move in moves:
        move.start()
    s1, f2, f3, f4, b2, b3, b4, wt = prepared
    for move in moves:
        move.wait()
    win = jnp.concatenate([win_ref[...], jnp.zeros((4, 128), F32)], axis=0)
    high = win.astype(BF16).astype(F32)
    s1[...] = jnp.concatenate([high, high, win - high], axis=0).astype(BF16)
    for raw, ahead, back in ((w2_ref, f2, b2), (w3_ref, f3, b3), (w4_ref, f4, b4)):
        ahead[...] = stacked(raw[...].T)
        back[...] = stacked(raw[...])
    wt[...] = jnp.broadcast_to(vec[4:5], (128, 128)).T
    network_rows(x_ref, base, count, prepared, vec, outs)


def opening_call(base, count, last, initial, x, win, w2, w3, w4, vectors):
    return pl.pallas_call(
        functools.partial(opening_kernel, base, count),
        in_specs=[ANY] * 2 + [HBM] * 10,
        out_specs=[VMEM] * 19,
        out_shape=[jax.ShapeDtypeStruct(x.shape, F32),
                   jax.ShapeDtypeStruct((8, 128), F32)] + PREPARED + network_shapes(count),
        scratch_shapes=[pltpu.VMEM((12, 128), F32)] + [pltpu.VMEM((128, 128), F32)] * 3
        + [pltpu.SemaphoreType.DMA((10,))],
        compiler_params=pltpu.CompilerParams(vmem_limit_bytes=LIMIT),
        cost_estimate=cost(count),
        name="network_first",
    )(last, initial, *pinned(x, win, w2, w3, w4, *vectors))


def middle_kernel(base, count, token, x_ref, *rest):
    network_rows(x_ref, base, count, rest[:8], rest[8], rest[9:])


def middle_call(base, count, token, x, prepared, vectors):
    return pl.pallas_call(
        functools.partial(middle_kernel, base, count),
        in_specs=[ANY] + [VMEM] * 10,
        out_specs=[VMEM] * 9,
        out_shape=network_shapes(count),
        compiler_params=pltpu.CompilerParams(vmem_limit_bytes=LIMIT),
        cost_estimate=cost(count),
        name="network",
    )(token, x, *prepared, vectors)


def packed(up_ref, inv_ref, cpl_ref, mis_ref, down_ref, out_ref, offset):
    rows = mis_ref.shape[1]
    tiles = rows // 8 + 2
    lane = lax.broadcasted_iota(jnp.int32, (8, 128), 1)
    for t in range(tiles):
        for j in range(3):
            out = jnp.zeros((8, 128), F32)
            for k in range(min(16, 46 - 16 * j)):
                value = tile_of(up_ref, inv_ref, cpl_ref, mis_ref, down_ref, 16 * j + k, t)
                by = (8 * k - offset) % 128
                here = (lane >= 8 * k) & (lane < 8 * k + 8)
                out = jnp.where(here, pltpu.roll(value, by, 1) if by else value, out)
            out_ref[j, pl.ds(8 * t, 8)] = out


def tile_of(up_ref, inv_ref, cpl_ref, mis_ref, down_ref, a, t):
    if t == 0:
        return up_ref[a]
    if t == mis_ref.shape[1] // 8 + 1:
        return down_ref[a]
    at = pl.ds(8 * (t - 1), 8)
    if a < 36:
        return inv_ref[a, at]
    return cpl_ref[a - 36, at] if a < 40 else mis_ref[a - 40, at]


def right_kernel(up_ref, inv_ref, cpl_ref, mis_ref, down_ref, token, out_ref):
    packed(up_ref, inv_ref, cpl_ref, mis_ref, down_ref, out_ref, 120)


def right_call(up, inv, cpl, mis, down, token):
    rows = mis.shape[1]
    return pl.pallas_call(
        right_kernel,
        in_specs=[VMEM] * 5 + [ANY],
        out_specs=VMEM,
        out_shape=jax.ShapeDtypeStruct((3, rows + 16, 128), F32),
        compiler_params=pltpu.CompilerParams(vmem_limit_bytes=LIMIT),
        name="right_columns",
    )(up, inv, cpl, mis, down, token)


def third_kernel(base, count, up_ref, inv_ref, cpl_ref, mis_ref, down_ref, x_ref, *rest):
    network_rows(x_ref, base, count, rest[:8], rest[8], rest[10:])
    packed(up_ref, inv_ref, cpl_ref, mis_ref, down_ref, rest[9], 0)


def third_call(base, count, up, inv, cpl, mis, down, x, prepared, vectors):
    rows = mis.shape[1]
    return pl.pallas_call(
        functools.partial(third_kernel, base, count),
        in_specs=[VMEM] * 15,
        out_specs=[VMEM] * 10,
        out_shape=[jax.ShapeDtypeStruct((3, rows + 16, 128), F32)] + network_shapes(count),
        compiler_params=pltpu.CompilerParams(vmem_limit_bytes=LIMIT),
        cost_estimate=cost(count),
        name="network_left",
    )(up, inv, cpl, mis, down, x, *prepared, vectors)


def final_kernel(up_ref, inv_ref, cpl_ref, mis_ref, down_ref, prod_ref, froml_ref, fromr_ref, wt, *rest):
    parts = [rest[9 * p : 9 * p + 9] for p in range(PARTS)]
    adj_ref, sens_ref, corr_ref, sums_ref, ext, main, side, acc4, acc3, acc2, acc1, flat = rest[9 * PARTS :]
    rows = mis_ref.shape[1]
    tiles = rows // 8 + 2
    lane = lax.broadcasted_iota(jnp.int32, (8, 128), 1)
    first, last = lane == 0, lane == 127

    def tile(a, t):
        return tile_of(up_ref, inv_ref, cpl_ref, mis_ref, down_ref, a, t)

    for a in range(46):
        j, k = a // 16, a % 16
        for t in range(tiles):
            at = pl.ds(8 * t, 8)
            high = fromr_ref[j, at]
            low = froml_ref[j, at]
            high = pltpu.roll(high, (128 - 8 * k) % 128, 1) if k else high
            low = pltpu.roll(low, 120 - 8 * k, 1) if k != 15 else low
            ext[a, at] = jnp.where(lane < 8, high, jnp.where(lane >= 120, low, 0.0))

    edge = jnp.zeros((8, 128), F32)
    for field in (main, side):
        for s in range(2):
            for i in range(6):
                field[s, i, 0:8] = edge
                field[s, i, pl.ds(8 * tiles + 8, 8)] = edge

    def solve(field, s, t, coefficient, rhs):
        for i in range(6):
            total = coefficient(6 * i) * rhs[0]
            for j in range(1, 6):
                total = total + coefficient(6 * i + j) * rhs[j]
            field[s, i, pl.ds(8 * t + 8, 8)] = total

    for t in range(tiles):
        at = pl.ds(8 * t, 8)
        solve(main, 0, t, lambda a: tile(a, t), [tile(40 + i, t) for i in range(6)])
        solve(side, 0, t, lambda a: ext[a, at], [ext[40 + i, at] for i in range(6)])

    def sweep(n, carry):
        s = lax.rem(n, 2)
        for t in range(tiles):
            at = pl.ds(8 * t, 8)
            near, beside = [], []
            for i in range(6):
                m = main[s, i, pl.ds(8 * t + 8, 8)]
                e = side[s, i, pl.ds(8 * t + 8, 8)]
                m_low, m_high = pltpu.roll(m, 1, 1), pltpu.roll(m, 127, 1)
                e_low, e_high = pltpu.roll(e, 1, 1), pltpu.roll(e, 127, 1)
                rhs = tile(40 + i, t) + tile(36, t) * main[s, i, pl.ds(8 * t + 7, 8)]
                rhs = rhs + tile(37, t) * main[s, i, pl.ds(8 * t + 9, 8)]
                rhs = rhs + tile(38, t) * jnp.where(first, e_low, m_low)
                near.append(rhs + tile(39, t) * jnp.where(last, e_high, m_high))
                rhs = ext[40 + i, at] + ext[36, at] * side[s, i, pl.ds(8 * t + 7, 8)]
                rhs = rhs + ext[37, at] * side[s, i, pl.ds(8 * t + 9, 8)]
                rhs = rhs + ext[38, at] * jnp.where(first, m_low, e_low)
                beside.append(rhs + ext[39, at] * jnp.where(last, m_high, e_high))
            solve(main, 1 - s, t, lambda a: tile(a, t), near)
            solve(side, 1 - s, t, lambda a: ext[a, at], beside)
        return carry

    lax.fori_loop(0, SWEEPS - 1, sweep, 0)
    done = (SWEEPS - 1) % 2

    square = jnp.zeros((8, 128), F32)
    for t in range(rows // 8):
        at = pl.ds(8 * t, 8)
        total = jnp.zeros((8, 128), F32)
        for i in range(6):
            value = main[done, i, pl.ds(8 * t + 16, 8)]
            adj_ref[i, at] = value
            total = total + value * prod_ref[i, at]
        sens_ref[at] = -total
        square = square + total * total

    for acc in (acc4, acc3, acc2, acc1):
        acc[...] = jnp.zeros_like(acc)
    flat[...] = jnp.zeros_like(flat)

    def term(scaled, right, acc, slot):
        total = flat[slot]
        pieces = []
        for value in scaled:
            total = total + value
            high, low = split(value)
            pieces.append(jnp.concatenate([high, low], axis=0))
        flat[slot] = total
        left = jnp.concatenate(pieces, axis=1)
        acc[...] += jnp.dot(left, right.reshape(128 * len(pieces), right.shape[2]), preferred_element_type=F32)

    base = 0
    for part in parts:
        corr, l1 = part[0], part[2]
        for r in range(corr.shape[0]):
            corr_ref[base + r : base + r + 1] = corr[r]

        def gather(g, carry, base=base, part=part):
            _, xc, l1, l2, l3, l4t, d3t, d2t, d1t = part
            at = WIDE * g
            some = pl.ds(at, WIDE)
            weights = [sens_ref[pl.ds(base + at + r, 1), :] for r in range(WIDE)]
            out = flat[4]
            scaled = []
            for r in range(WIDE):
                value = l4t[at + r]
                out = out + value * weights[r]
                scaled.append(wt[...] * (1.0 - value * value) * weights[r])
            flat[4] = out
            term(scaled, l3[some], acc4, 3)
            for delta, layer, acc, slot in ((d3t, l2, acc3, 2), (d2t, l1, acc2, 1), (d1t, xc, acc1, 0)):
                term([delta[at + r] * weights[r] for r in range(WIDE)], layer[some], acc, slot)
            return carry

        lax.fori_loop(0, l1.shape[0] // WIDE, gather, 0)
        base += l1.shape[0]

    for n, acc in enumerate((acc4, acc3, acc2)):
        sums_ref[pl.ds(128 * n, 128)] = (acc[0:128, 0:128] + acc[128:256, 0:128]) + (
            acc[0:128, 128:256] + acc[128:256, 128:256])
    lanes = lax.broadcasted_iota(jnp.int32, (128, 128), 1)
    block = jnp.zeros((128, 128), F32)
    for slot in range(5):
        block = jnp.where(lanes == 16 + slot, jnp.sum(flat[slot], axis=1, keepdims=True), block)
    block = jnp.where(lanes == 21, jnp.sum(square), block)
    own = acc1[0:128] + acc1[128:256]
    own = jnp.concatenate([own, jnp.zeros((128, 80), F32)], axis=1)
    own = own + pltpu.roll(own, 112, 1)
    sums_ref[pl.ds(384, 128)] = jnp.where(lanes < 12, own, block)


def final_call(up, inv, cpl, mis, down, prod, froml, fromr, wt, parts):
    rows = mis.shape[1]
    flat = [value for part in parts for value in part]
    return pl.pallas_call(
        final_kernel,
        in_specs=[VMEM] * (9 + len(flat)),
        out_specs=[VMEM] * 4,
        out_shape=[
            jax.ShapeDtypeStruct((6, rows, 128), F32),
            jax.ShapeDtypeStruct((rows, 128), F32),
            jax.ShapeDtypeStruct((rows, 128), F32),
            jax.ShapeDtypeStruct((512, 128), F32),
        ],
        scratch_shapes=[
            pltpu.VMEM((46, rows + 16, 128), F32),
            pltpu.VMEM((2, 6, rows + 32, 128), F32),
            pltpu.VMEM((2, 6, rows + 32, 128), F32),
            pltpu.VMEM((256, 256), F32),
            pltpu.VMEM((256, 256), F32),
            pltpu.VMEM((256, 256), F32),
            pltpu.VMEM((256, 48), F32),
            pltpu.VMEM((5, 128, 128), F32),
        ],
        compiler_params=pltpu.CompilerParams(vmem_limit_bytes=LIMIT),
        name="final",
    )(up, inv, cpl, mis, down, prod, froml, fromr, wt, *flat)


def unpack_kernel(sums_ref, w4_ref, w3_ref, w2_ref, win_ref, b1_ref, b2_ref, b3_ref, b4_ref, out_ref):
    block = sums_ref[pl.ds(384, 128)]
    scale = 1.0 / jnp.sqrt(jnp.broadcast_to(block[0:1, 21:22], (1, 128)) + EPS)
    for n, ref in enumerate((w4_ref, w3_ref, w2_ref)):
        ref[...] = sums_ref[pl.ds(128 * n, 128)] * scale
    block = block * scale
    turned = block.T
    win_ref[...] = turned[0:12]
    for n, ref in enumerate((b1_ref, b2_ref, b3_ref, b4_ref, out_ref)):
        ref[...] = turned[16 + n : 17 + n]


def unpack_call(sums):
    shapes = [(128, 128)] * 3 + [(12, 128)] + [(1, 128)] * 5
    return pl.pallas_call(
        unpack_kernel,
        in_specs=[VMEM],
        out_shape=[jax.ShapeDtypeStruct(shape, F32) for shape in shapes],
        compiler_params=pltpu.CompilerParams(vmem_limit_bytes=2 * MIB),
        name="unpack",
    )(sums)


def sent(value, axes, wrap, by):
    size = lax.axis_size(axes)
    pairs = [(i, (i + by) % size) for i in range(size) if wrap or 0 <= i + by < size]
    return lax.ppermute(value, axes, pairs)


def summed(value):
    near, far = lax.axis_size(NEAR), lax.axis_size(FAR)
    rows = value.shape[0] // near
    part = lax.all_to_all(value.reshape(near, rows, 128), NEAR, 0, 0)
    part = jnp.sum(part, axis=0)
    part = lax.all_to_all(jnp.broadcast_to(part[None], (far, rows, 128)), FAR, 0, 0)
    part = jnp.sum(part, axis=0)
    whole = lax.all_to_all(jnp.broadcast_to(part[None], (near, rows, 128)), NEAR, 0, 0)
    return whole.reshape(near * rows, 128)


def local(features, inverse_diag, couplings, mismatch, production, weight_in, bias_in, weight_two,
          bias_two, weight_three, bias_three, weight_four, bias_four, weight_out):
    nvars, rows, cols = mismatch.shape
    inverse = inverse_diag.reshape(nvars * nvars, rows, cols)
    win = weight_in.T
    vectors = [v.reshape(1, 128) for v in (bias_in, bias_two, bias_three, bias_four, weight_out)]
    count = rows // PARTS

    last, initial = edge_call(inverse, couplings, mismatch)
    above = sent(last, SUB, False, 1)
    below = sent(initial, SUB, False, -1)
    features, vectors, *rest = opening_call(
        0, count, last, initial, features, win, weight_two, weight_three, weight_four, vectors)
    prepared, first = rest[:8], rest[8:]
    second = middle_call(count, count, first[0], features, prepared, vectors)

    right = right_call(above, inverse, couplings, mismatch, below, second[0])
    from_low = sent(right, BLK, True, 1)
    left, *third = third_call(2 * count, count, above, inverse, couplings, mismatch, below, features,
                              prepared, vectors)
    from_high = sent(left, BLK, True, -1)
    fourth = middle_call(3 * count, count, from_low, features, prepared, vectors)

    parts = (first, second, third, fourth)
    adjoint, sensitivity, correction, sums = final_call(
        above, inverse, couplings, mismatch, below, production, from_low, from_high, prepared[7],
        parts)
    g4, g3, g2, gin, b1, b2, b3, b4, gout = unpack_call(summed(sums))
    flat = lambda value: value.reshape(128)
    return (adjoint, sensitivity, correction, gin.T, flat(b1), g2, flat(b2),
            g3, flat(b3), g4, flat(b4), flat(gout))


def solution(mesh):
    sizes = (16, 2, 2, 4, 2) if mesh.devices.size == 512 else (mesh.shape["blk"], 1, 1, mesh.shape["sub"], 1)
    fine = Mesh(mesh.devices.reshape(sizes), BLK + SUB)
    three = P(None, SUB, BLK)
    two = P(SUB, BLK)
    return jax.shard_map(
        local,
        mesh=fine,
        in_specs=(three, P(None, None, SUB, BLK), three, three, three) + (P(),) * 9,
        out_specs=(three, two, two) + (P(),) * 9,
        check_vma=False,
    )
```

```python
import functools
import jax
import jax.numpy as jnp
from jax import lax
from jax.experimental import pallas as pl
from jax.experimental.pallas import tpu as pltpu
from jax.sharding import Mesh, PartitionSpec as P

SWEEPS = 8
EPS = 1e-06
BLK = ("z", "xh", "c")
SUB = ("y", "xl")
NEAR = ("xh", "c", "y", "xl")
FAR = ("z",)
F32 = jnp.float32
BF16 = jnp.bfloat16
GROUP = 8
WIDE = 8
PARTS = 3
MIB = 1 << 20
LIMIT = 8 * MIB


def split(value):
    high = value.astype(BF16)
    return high, (value - high.astype(F32)).astype(BF16)


def pair(value):
    return jnp.concatenate(split(value), axis=1)


def joined(both):
    return both[:, :128].astype(F32) + both[:, 128:].astype(F32)


def times(both, weights):
    out = jnp.dot(both, weights, preferred_element_type=F32)
    return out[:, :128] + out[:, 128:]


def stacked(weight):
    both = pair(weight)
    return jnp.concatenate([both, both], axis=0)


VMEM = pl.BlockSpec(memory_space=pltpu.VMEM)
ANY = pl.BlockSpec(memory_space=pl.ANY)
HBM = pl.BlockSpec(memory_space=pltpu.MemorySpace.HBM)


def network_rows(x_ref, base, count, prepared, vectors, outs):
    s1, f2, f3, f4, b2, b3, b4, wt = prepared
    bias1, bias2, bias3, bias4, wout = (vectors.at[pl.ds(n, 1)] for n in range(5))
    corr_ref, xc_ref, l1_ref, l2_ref, l3_ref, l4t_ref, d3t_ref, d2t_ref, d1t_ref = outs
    pad = jnp.zeros((4, 128), F32)

    def step(g, carry):
        at = GROUP * g
        columns = []
        for r in range(GROUP):
            x = jnp.concatenate([x_ref[:, base + at + r, :], pad], axis=0)
            high = x.astype(BF16).astype(F32)
            column = jnp.concatenate([high, x - high, high], axis=0).T.astype(BF16)
            xc_ref[at + r] = column
            columns.append(column)
        inputs = jnp.concatenate(columns, axis=0)
        layer = jnp.tanh(jnp.dot(inputs, s1[...], preferred_element_type=F32) + bias1[...])
        layers = []
        for out, weights, bias in ((l1_ref, f2, bias2), (l2_ref, f3, bias3), (l3_ref, f4, bias4)):
            layers.append(layer)
            both = pair(layer)
            out[pl.ds(at, GROUP)] = both.reshape(GROUP, 128, 256)
            layer = jnp.tanh(times(both, weights[...]) + bias[...])
        for r in range(GROUP):
            turned = layer[128 * r : 128 * r + 128].T
            l4t_ref[at + r] = turned
            corr_ref[at + r] = 1.0 + jnp.sum(turned * wt[...], axis=0, keepdims=True)
        delta = wout[...] * (1.0 - layer * layer)
        for weights, out in ((b4, d3t_ref), (b3, d2t_ref), (b2, d1t_ref)):
            layer = layers.pop()
            delta = times(pair(delta), weights[...]) * (1.0 - layer * layer)
            for r in range(GROUP):
                out[at + r] = delta[128 * r : 128 * r + 128].T
        return carry

    lax.fori_loop(0, count // GROUP, step, 0)


def network_shapes(count):
    return [
        jax.ShapeDtypeStruct((count, 1, 128), F32),
        jax.ShapeDtypeStruct((count, 128, 48), BF16),
    ] + [jax.ShapeDtypeStruct((count, 128, 256), BF16)] * 3 + [jax.ShapeDtypeStruct((count, 128, 128), F32)] * 4


PREPARED = [jax.ShapeDtypeStruct((48, 128), BF16)] + [jax.ShapeDtypeStruct((256, 256), BF16)] * 6 + [
    jax.ShapeDtypeStruct((128, 128), F32)]


def cost(count):
    return pl.CostEstimate(flops=count * 3 * 10**8, bytes_accessed=count * 1000, transcendentals=0)


def strips(fields, out, row, sem):
    moves, at = [], 0
    for i, field in enumerate(fields):
        n = field.shape[0]
        moves.append(pltpu.make_async_copy(field.at[:, pl.ds(row, 8)], out.at[pl.ds(at, n)], sem.at[i]))
        at += n
    for move in moves:
        move.start()
    return moves


def pinned(*values):
    return [pltpu.with_memory_space_constraint(value, pltpu.MemorySpace.HBM) for value in values]


def edge_kernel(inv_hbm, cpl_hbm, mis_hbm, last, initial, sem):
    rows = mis_hbm.shape[1]
    fields = (inv_hbm, cpl_hbm, mis_hbm)
    moves = strips(fields, last, rows - 8, sem.at[0]) + strips(fields, initial, 0, sem.at[1])
    for move in moves:
        move.wait()


def edge_call(inv, cpl, mis):
    return pl.pallas_call(
        edge_kernel,
        in_specs=[HBM] * 3,
        out_specs=[ANY] * 2,
        out_shape=[jax.ShapeDtypeStruct((46, 8, 128), F32)] * 2,
        scratch_shapes=[pltpu.SemaphoreType.DMA((2, 3))],
        compiler_params=pltpu.CompilerParams(vmem_limit_bytes=MIB),
        name="edge_rows",
    )(*pinned(inv, cpl, mis))


def opening_kernel(base, count, last_hbm, first_hbm, x_hbm, win_hbm, w2_hbm, w3_hbm, w4_hbm, *rest):
    vectors, rest = rest[:5], rest[5:]
    x_ref, vec, prepared, outs = rest[0], rest[1], rest[2:10], rest[10:19]
    win_ref, w2_ref, w3_ref, w4_ref, sem = rest[19:]
    moves = [
        pltpu.make_async_copy(source, target, sem.at[i])
        for i, (source, target) in enumerate(
            [(w2_hbm, w2_ref), (w3_hbm, w3_ref), (w4_hbm, w4_ref), (win_hbm, win_ref), (x_hbm, x_ref)]
            + [(vector, vec.at[pl.ds(n, 1)]) for n, vector in enumerate(vectors)])
    ]
    for move in moves:
        move.start()
    s1, f2, f3, f4, b2, b3, b4, wt = prepared
    for move in moves:
        move.wait()
    win = jnp.concatenate([win_ref[...], jnp.zeros((4, 128), F32)], axis=0)
    high = win.astype(BF16).astype(F32)
    s1[...] = jnp.concatenate([high, high, win - high], axis=0).astype(BF16)
    for raw, ahead, back in ((w2_ref, f2, b2), (w3_ref, f3, b3), (w4_ref, f4, b4)):
        ahead[...] = stacked(raw[...].T)
        back[...] = stacked(raw[...])
    wt[...] = jnp.broadcast_to(vec[4:5], (128, 128)).T
    network_rows(x_ref, base, count, prepared, vec, outs)


def opening_call(base, count, last, initial, x, win, w2, w3, w4, vectors):
    return pl.pallas_call(
        functools.partial(opening_kernel, base, count),
        in_specs=[ANY] * 2 + [HBM] * 10,
        out_specs=[VMEM] * 19,
        out_shape=[jax.ShapeDtypeStruct(x.shape, F32),
                   jax.ShapeDtypeStruct((8, 128), F32)] + PREPARED + network_shapes(count),
        scratch_shapes=[pltpu.VMEM((12, 128), F32)] + [pltpu.VMEM((128, 128), F32)] * 3
        + [pltpu.SemaphoreType.DMA((10,))],
        compiler_params=pltpu.CompilerParams(vmem_limit_bytes=LIMIT),
        cost_estimate=cost(count),
        name="network_first",
    )(last, initial, *pinned(x, win, w2, w3, w4, *vectors))


def middle_kernel(base, count, token, x_ref, *rest):
    network_rows(x_ref, base, count, rest[:8], rest[8], rest[9:])


def middle_call(base, count, token, x, prepared, vectors):
    return pl.pallas_call(
        functools.partial(middle_kernel, base, count),
        in_specs=[ANY] + [VMEM] * 10,
        out_specs=[VMEM] * 9,
        out_shape=network_shapes(count),
        compiler_params=pltpu.CompilerParams(vmem_limit_bytes=LIMIT),
        cost_estimate=cost(count),
        name="network",
    )(token, x, *prepared, vectors)


def packed(up_ref, inv_ref, cpl_ref, mis_ref, down_ref, out_ref, offset):
    rows = mis_ref.shape[1]
    tiles = rows // 8 + 2
    lane = lax.broadcasted_iota(jnp.int32, (8, 128), 1)
    for t in range(tiles):
        for j in range(3):
            out = jnp.zeros((8, 128), F32)
            for k in range(min(16, 46 - 16 * j)):
                value = tile_of(up_ref, inv_ref, cpl_ref, mis_ref, down_ref, 16 * j + k, t)
                by = (8 * k - offset) % 128
                here = (lane >= 8 * k) & (lane < 8 * k + 8)
                out = jnp.where(here, pltpu.roll(value, by, 1) if by else value, out)
            out_ref[j, pl.ds(8 * t, 8)] = out


def tile_of(up_ref, inv_ref, cpl_ref, mis_ref, down_ref, a, t):
    if t == 0:
        return up_ref[a]
    if t == mis_ref.shape[1] // 8 + 1:
        return down_ref[a]
    at = pl.ds(8 * (t - 1), 8)
    if a < 36:
        return inv_ref[a, at]
    return cpl_ref[a - 36, at] if a < 40 else mis_ref[a - 40, at]


def right_kernel(up_ref, inv_ref, cpl_ref, mis_ref, down_ref, token, out_ref):
    packed(up_ref, inv_ref, cpl_ref, mis_ref, down_ref, out_ref, 120)


def right_call(up, inv, cpl, mis, down, token):
    rows = mis.shape[1]
    return pl.pallas_call(
        right_kernel,
        in_specs=[VMEM] * 5 + [ANY],
        out_specs=VMEM,
        out_shape=jax.ShapeDtypeStruct((3, rows + 16, 128), F32),
        compiler_params=pltpu.CompilerParams(vmem_limit_bytes=LIMIT),
        name="right_columns",
    )(up, inv, cpl, mis, down, token)


def third_kernel(base, count, up_ref, inv_ref, cpl_ref, mis_ref, down_ref, x_ref, *rest):
    network_rows(x_ref, base, count, rest[:8], rest[8], rest[10:])
    packed(up_ref, inv_ref, cpl_ref, mis_ref, down_ref, rest[9], 0)


def third_call(base, count, up, inv, cpl, mis, down, x, prepared, vectors):
    rows = mis.shape[1]
    return pl.pallas_call(
        functools.partial(third_kernel, base, count),
        in_specs=[VMEM] * 15,
        out_specs=[VMEM] * 10,
        out_shape=[jax.ShapeDtypeStruct((3, rows + 16, 128), F32)] + network_shapes(count),
        compiler_params=pltpu.CompilerParams(vmem_limit_bytes=LIMIT),
        cost_estimate=cost(count),
        name="network_left",
    )(up, inv, cpl, mis, down, x, *prepared, vectors)


def final_kernel(up_ref, inv_ref, cpl_ref, mis_ref, down_ref, prod_ref, froml_ref, fromr_ref, wt, *rest):
    parts = [rest[9 * p : 9 * p + 9] for p in range(PARTS)]
    adj_ref, sens_ref, corr_ref, sums_ref, ext, *rest = rest[9 * PARTS :]
    main, side, (acc4, acc3, acc2, acc1, flat) = rest[0:2], rest[2:4], rest[4:]
    rows = mis_ref.shape[1]
    tiles = rows // 8 + 2
    lane = lax.broadcasted_iota(jnp.int32, (8, 128), 1)
    first, last = lane == 0, lane == 127

    def tile(a, t):
        return tile_of(up_ref, inv_ref, cpl_ref, mis_ref, down_ref, a, t)

    for a in range(46):
        j, k = a // 16, a % 16
        for t in range(tiles):
            at = pl.ds(8 * t, 8)
            high = fromr_ref[j, at]
            low = froml_ref[j, at]
            high = pltpu.roll(high, (128 - 8 * k) % 128, 1) if k else high
            low = pltpu.roll(low, 120 - 8 * k, 1) if k != 15 else low
            ext[a, at] = jnp.where(lane < 8, high, jnp.where(lane >= 120, low, 0.0))

    edge = jnp.zeros((8, 128), F32)
    for field in main + side:
        for i in range(6):
            field[i, 0:8] = edge
            field[i, pl.ds(8 * tiles + 8, 8)] = edge

    def solve(field, t, coefficient, rhs):
        for i in range(6):
            total = coefficient(6 * i) * rhs[0]
            for j in range(1, 6):
                total = total + coefficient(6 * i + j) * rhs[j]
            field[i, pl.ds(8 * t + 8, 8)] = total

    for t in range(tiles):
        at = pl.ds(8 * t, 8)
        solve(main[0], t, lambda a: tile(a, t), [tile(40 + i, t) for i in range(6)])
        solve(side[0], t, lambda a: ext[a, at], [ext[40 + i, at] for i in range(6)])

    def sweep(main, side, main_next, side_next):
        for t in range(tiles):
            at = pl.ds(8 * t, 8)
            near, beside = [], []
            for i in range(6):
                m = main[i, pl.ds(8 * t + 8, 8)]
                e = side[i, pl.ds(8 * t + 8, 8)]
                m_low, m_high = pltpu.roll(m, 1, 1), pltpu.roll(m, 127, 1)
                e_low, e_high = pltpu.roll(e, 1, 1), pltpu.roll(e, 127, 1)
                rhs = tile(40 + i, t) + tile(36, t) * main[i, pl.ds(8 * t + 7, 8)]
                rhs = rhs + tile(37, t) * main[i, pl.ds(8 * t + 9, 8)]
                rhs = rhs + tile(38, t) * jnp.where(first, e_low, m_low)
                near.append(rhs + tile(39, t) * jnp.where(last, e_high, m_high))
                rhs = ext[40 + i, at] + ext[36, at] * side[i, pl.ds(8 * t + 7, 8)]
                rhs = rhs + ext[37, at] * side[i, pl.ds(8 * t + 9, 8)]
                rhs = rhs + ext[38, at] * jnp.where(first, m_low, e_low)
                beside.append(rhs + ext[39, at] * jnp.where(last, m_high, e_high))
            solve(main_next, t, lambda a: tile(a, t), near)
            solve(side_next, t, lambda a: ext[a, at], beside)

    def two(n, carry):
        sweep(main[0], side[0], main[1], side[1])
        sweep(main[1], side[1], main[0], side[0])
        return carry

    lax.fori_loop(0, (SWEEPS - 1) // 2, two, 0)
    if (SWEEPS - 1) % 2:
        sweep(main[0], side[0], main[1], side[1])
    done = main[(SWEEPS - 1) % 2]

    square = jnp.zeros((8, 128), F32)
    for t in range(rows // 8):
        at = pl.ds(8 * t, 8)
        total = jnp.zeros((8, 128), F32)
        for i in range(6):
            value = done[i, pl.ds(8 * t + 16, 8)]
            adj_ref[i, at] = value
            total = total + value * prod_ref[i, at]
        sens_ref[at] = -total
        square = square + total * total

    for acc in (acc4, acc3, acc2, acc1):
        acc[...] = jnp.zeros_like(acc)
    flat[...] = jnp.zeros_like(flat)

    def term(scaled, right, acc, slot):
        total = flat[slot]
        pieces = []
        for value in scaled:
            total = total + value
            high, low = split(value)
            pieces.append(jnp.concatenate([high, low], axis=0))
        flat[slot] = total
        left = jnp.concatenate(pieces, axis=1)
        acc[...] += jnp.dot(left, right.reshape(128 * len(pieces), right.shape[2]), preferred_element_type=F32)

    base = 0
    for part in parts:
        corr, l1 = part[0], part[2]
        for r in range(corr.shape[0]):
            corr_ref[base + r : base + r + 1] = corr[r]

        def gather(g, carry, base=base, part=part):
            _, xc, l1, l2, l3, l4t, d3t, d2t, d1t = part
            at = WIDE * g
            some = pl.ds(at, WIDE)
            weights = [sens_ref[pl.ds(base + at + r, 1), :] for r in range(WIDE)]
            out = flat[4]
            scaled = []
            for r in range(WIDE):
                value = l4t[at + r]
                out = out + value * weights[r]
                scaled.append(wt[...] * (1.0 - value * value) * weights[r])
            flat[4] = out
            term(scaled, l3[some], acc4, 3)
            for delta, layer, acc, slot in ((d3t, l2, acc3, 2), (d2t, l1, acc2, 1), (d1t, xc, acc1, 0)):
                term([delta[at + r] * weights[r] for r in range(WIDE)], layer[some], acc, slot)
            return carry

        lax.fori_loop(0, l1.shape[0] // WIDE, gather, 0)
        base += l1.shape[0]

    for n, acc in enumerate((acc4, acc3, acc2)):
        sums_ref[pl.ds(128 * n, 128)] = (acc[0:128, 0:128] + acc[128:256, 0:128]) + (
            acc[0:128, 128:256] + acc[128:256, 128:256])
    lanes = lax.broadcasted_iota(jnp.int32, (128, 128), 1)
    block = jnp.zeros((128, 128), F32)
    for slot in range(5):
        block = jnp.where(lanes == 16 + slot, jnp.sum(flat[slot], axis=1, keepdims=True), block)
    block = jnp.where(lanes == 21, jnp.sum(square), block)
    own = acc1[0:128] + acc1[128:256]
    own = jnp.concatenate([own, jnp.zeros((128, 80), F32)], axis=1)
    own = own + pltpu.roll(own, 112, 1)
    sums_ref[pl.ds(384, 128)] = jnp.where(lanes < 12, own, block)


def final_call(up, inv, cpl, mis, down, prod, froml, fromr, wt, parts):
    rows = mis.shape[1]
    flat = [value for part in parts for value in part]
    return pl.pallas_call(
        final_kernel,
        in_specs=[VMEM] * (9 + len(flat)),
        out_specs=[VMEM] * 4,
        out_shape=[
            jax.ShapeDtypeStruct((6, rows, 128), F32),
            jax.ShapeDtypeStruct((rows, 128), F32),
            jax.ShapeDtypeStruct((rows, 128), F32),
            jax.ShapeDtypeStruct((512, 128), F32),
        ],
        scratch_shapes=[
            pltpu.VMEM((46, rows + 16, 128), F32),
            pltpu.VMEM((6, rows + 32, 128), F32),
            pltpu.VMEM((6, rows + 32, 128), F32),
            pltpu.VMEM((6, rows + 32, 128), F32),
            pltpu.VMEM((6, rows + 32, 128), F32),
            pltpu.VMEM((256, 256), F32),
            pltpu.VMEM((256, 256), F32),
            pltpu.VMEM((256, 256), F32),
            pltpu.VMEM((256, 48), F32),
            pltpu.VMEM((5, 128, 128), F32),
        ],
        compiler_params=pltpu.CompilerParams(vmem_limit_bytes=LIMIT),
        name="final",
    )(up, inv, cpl, mis, down, prod, froml, fromr, wt, *flat)


def unpack_kernel(sums_ref, w4_ref, w3_ref, w2_ref, win_ref, b1_ref, b2_ref, b3_ref, b4_ref, out_ref):
    block = sums_ref[pl.ds(384, 128)]
    scale = 1.0 / jnp.sqrt(jnp.broadcast_to(block[0:1, 21:22], (1, 128)) + EPS)
    for n, ref in enumerate((w4_ref, w3_ref, w2_ref)):
        ref[...] = sums_ref[pl.ds(128 * n, 128)] * scale
    block = block * scale
    turned = block.T
    win_ref[...] = turned[0:12]
    for n, ref in enumerate((b1_ref, b2_ref, b3_ref, b4_ref, out_ref)):
        ref[...] = turned[16 + n : 17 + n]


def unpack_call(sums):
    shapes = [(128, 128)] * 3 + [(12, 128)] + [(1, 128)] * 5
    return pl.pallas_call(
        unpack_kernel,
        in_specs=[VMEM],
        out_shape=[jax.ShapeDtypeStruct(shape, F32) for shape in shapes],
        compiler_params=pltpu.CompilerParams(vmem_limit_bytes=2 * MIB),
        name="unpack",
    )(sums)


def sent(value, axes, wrap, by):
    size = lax.axis_size(axes)
    pairs = [(i, (i + by) % size) for i in range(size) if wrap or 0 <= i + by < size]
    return lax.ppermute(value, axes, pairs)


def summed(value):
    near, far = lax.axis_size(NEAR), lax.axis_size(FAR)
    rows = value.shape[0] // near
    part = lax.all_to_all(value.reshape(near, rows, 128), NEAR, 0, 0)
    part = jnp.sum(part, axis=0)
    part = lax.all_to_all(jnp.broadcast_to(part[None], (far, rows, 128)), FAR, 0, 0)
    part = jnp.sum(part, axis=0)
    whole = lax.all_to_all(jnp.broadcast_to(part[None], (near, rows, 128)), NEAR, 0, 0)
    return whole.reshape(near * rows, 128)


def local(features, inverse_diag, couplings, mismatch, production, weight_in, bias_in, weight_two,
          bias_two, weight_three, bias_three, weight_four, bias_four, weight_out):
    nvars, rows, cols = mismatch.shape
    inverse = inverse_diag.reshape(nvars * nvars, rows, cols)
    win = weight_in.T
    vectors = [v.reshape(1, 128) for v in (bias_in, bias_two, bias_three, bias_four, weight_out)]
    count = rows // 4

    last, initial = edge_call(inverse, couplings, mismatch)
    above = sent(last, SUB, False, 1)
    below = sent(initial, SUB, False, -1)
    features, vectors, *rest = opening_call(
        0, 2 * count, last, initial, features, win, weight_two, weight_three, weight_four, vectors)
    prepared, first = rest[:8], rest[8:]

    right = right_call(above, inverse, couplings, mismatch, below, first[0])
    from_low = sent(right, BLK, True, 1)
    left, *second = third_call(2 * count, count, above, inverse, couplings, mismatch, below, features,
                              prepared, vectors)
    from_high = sent(left, BLK, True, -1)
    third = middle_call(3 * count, count, from_low, features, prepared, vectors)

    parts = (first, second, third)
    adjoint, sensitivity, correction, sums = final_call(
        above, inverse, couplings, mismatch, below, production, from_low, from_high, prepared[7],
        parts)
    g4, g3, g2, gin, b1, b2, b3, b4, gout = unpack_call(summed(sums))
    flat = lambda value: value.reshape(128)
    return (adjoint, sensitivity, correction, gin.T, flat(b1), g2, flat(b2),
            g3, flat(b3), g4, flat(b4), flat(gout))


def solution(mesh):
    sizes = (16, 2, 2, 4, 2) if mesh.devices.size == 512 else (mesh.shape["blk"], 1, 1, mesh.shape["sub"], 1)
    fine = Mesh(mesh.devices.reshape(sizes), BLK + SUB)
    three = P(None, SUB, BLK)
    two = P(SUB, BLK)
    return jax.shard_map(
        local,
        mesh=fine,
        in_specs=(three, P(None, None, SUB, BLK), three, three, three) + (P(),) * 9,
        out_specs=(three, two, two) + (P(),) * 9,
        check_vma=False,
    )
```

```python
import functools
import jax
import jax.numpy as jnp
from jax import lax
from jax.experimental import pallas as pl
from jax.experimental.pallas import tpu as pltpu
from jax.sharding import Mesh, PartitionSpec as P

SWEEPS = 8
EPS = 1e-06
BLK = ("z", "xh", "c")
SUB = ("y", "xl")
NEAR = ("xh", "c", "y", "xl")
FAR = ("z",)
F32 = jnp.float32
BF16 = jnp.bfloat16
GROUP = 8
PARTS = 3
MIB = 1 << 20
ROWS = 416
LIMIT = 8 * MIB


def split(value):
    high = value.astype(BF16)
    return high, (value - high.astype(F32)).astype(BF16)


def pair(value):
    return jnp.concatenate(split(value), axis=1)


def joined(both):
    return both[:, :128].astype(F32) + both[:, 128:].astype(F32)


def times(both, weights):
    out = jnp.dot(both, weights, preferred_element_type=F32)
    return out[:, :128] + out[:, 128:]


def stacked(weight):
    both = pair(weight)
    return jnp.concatenate([both, both], axis=0)


VMEM = pl.BlockSpec(memory_space=pltpu.VMEM)
ANY = pl.BlockSpec(memory_space=pl.ANY)
HBM = pl.BlockSpec(memory_space=pltpu.MemorySpace.HBM)


def network_rows(x_ref, base, count, prepared, vectors, outs):
    s1, f2, f3, f4, b2, b3, b4, wt = prepared
    bias1, bias2, bias3, bias4, wout = (vectors.at[pl.ds(n, 1)] for n in range(5))
    corr_ref, xc_ref, l1_ref, l2_ref, l3_ref, l4t_ref, d3t_ref, d2t_ref, d1t_ref = outs
    pad = jnp.zeros((4, 128), F32)

    def step(g, carry):
        at = GROUP * g
        columns = []
        for r in range(GROUP):
            x = jnp.concatenate([x_ref[:, base + at + r, :], pad], axis=0)
            high = x.astype(BF16).astype(F32)
            column = jnp.concatenate([high, x - high, high], axis=0).T.astype(BF16)
            xc_ref[at + r] = column
            columns.append(column)
        inputs = jnp.concatenate(columns, axis=0)
        layer = jnp.tanh(jnp.dot(inputs, s1[...], preferred_element_type=F32) + bias1[...])
        layers = []
        for out, weights, bias in ((l1_ref, f2, bias2), (l2_ref, f3, bias3), (l3_ref, f4, bias4)):
            layers.append(layer)
            both = pair(layer)
            out[pl.ds(at, GROUP)] = both.reshape(GROUP, 128, 256)
            layer = jnp.tanh(times(both, weights[...]) + bias[...])
        for r in range(GROUP):
            turned = layer[128 * r : 128 * r + 128].T
            l4t_ref[at + r] = turned
            corr_ref[at + r] = 1.0 + jnp.sum(turned * wt[...], axis=0, keepdims=True)
        delta = wout[...] * (1.0 - layer * layer)
        for weights, out in ((b4, d3t_ref), (b3, d2t_ref), (b2, d1t_ref)):
            layer = layers.pop()
            delta = times(pair(delta), weights[...]) * (1.0 - layer * layer)
            for r in range(GROUP):
                out[at + r] = delta[128 * r : 128 * r + 128].T
        return carry

    lax.fori_loop(0, count // GROUP, step, 0)


def network_shapes(count):
    return [
        jax.ShapeDtypeStruct((count, 1, 128), F32),
        jax.ShapeDtypeStruct((count, 128, 48), BF16),
    ] + [jax.ShapeDtypeStruct((count, 128, 256), BF16)] * 3 + [jax.ShapeDtypeStruct((count, 128, 128), F32)] * 4


PREPARED = [jax.ShapeDtypeStruct((48, 128), BF16)] + [jax.ShapeDtypeStruct((256, 256), BF16)] * 6 + [
    jax.ShapeDtypeStruct((128, 128), F32)]


def cost(count):
    return pl.CostEstimate(flops=count * 3 * 10**8, bytes_accessed=count * 1000, transcendentals=0)


def strips(fields, out, row, sem):
    moves, at = [], 0
    for i, field in enumerate(fields):
        n = field.shape[0]
        moves.append(pltpu.make_async_copy(field.at[:, pl.ds(row, 8)], out.at[pl.ds(at, n)], sem.at[i]))
        at += n
    for move in moves:
        move.start()
    return moves


def pinned(*values):
    return [pltpu.with_memory_space_constraint(value, pltpu.MemorySpace.HBM) for value in values]


def edge_kernel(inv_hbm, cpl_hbm, mis_hbm, last, initial, sem):
    rows = mis_hbm.shape[1]
    fields = (inv_hbm, cpl_hbm, mis_hbm)
    moves = strips(fields, last, rows - 8, sem.at[0]) + strips(fields, initial, 0, sem.at[1])
    for move in moves:
        move.wait()


def edge_call(inv, cpl, mis):
    return pl.pallas_call(
        edge_kernel,
        in_specs=[HBM] * 3,
        out_specs=[ANY] * 2,
        out_shape=[jax.ShapeDtypeStruct((46, 8, 128), F32)] * 2,
        scratch_shapes=[pltpu.SemaphoreType.DMA((2, 3))],
        compiler_params=pltpu.CompilerParams(vmem_limit_bytes=MIB),
        name="edge_rows",
    )(*pinned(inv, cpl, mis))


def opening_kernel(base, count, last_hbm, first_hbm, x_hbm, win_hbm, w2_hbm, w3_hbm, w4_hbm, *rest):
    vectors, rest = rest[:5], rest[5:]
    x_ref, vec, prepared, outs = rest[0], rest[1], rest[2:10], rest[10:19]
    win_ref, w2_ref, w3_ref, w4_ref, sem = rest[19:]
    moves = [
        pltpu.make_async_copy(source, target, sem.at[i])
        for i, (source, target) in enumerate(
            [(w2_hbm, w2_ref), (w3_hbm, w3_ref), (w4_hbm, w4_ref), (win_hbm, win_ref), (x_hbm, x_ref)]
            + [(vector, vec.at[pl.ds(n, 1)]) for n, vector in enumerate(vectors)])
    ]
    for move in moves:
        move.start()
    s1, f2, f3, f4, b2, b3, b4, wt = prepared
    for move in moves:
        move.wait()
    win = jnp.concatenate([win_ref[...], jnp.zeros((4, 128), F32)], axis=0)
    high = win.astype(BF16).astype(F32)
    s1[...] = jnp.concatenate([high, high, win - high], axis=0).astype(BF16)
    for raw, ahead, back in ((w2_ref, f2, b2), (w3_ref, f3, b3), (w4_ref, f4, b4)):
        ahead[...] = stacked(raw[...].T)
        back[...] = stacked(raw[...])
    wt[...] = jnp.broadcast_to(vec[4:5], (128, 128)).T
    network_rows(x_ref, base, count, prepared, vec, outs)


def opening_call(base, count, last, initial, x, win, w2, w3, w4, vectors):
    return pl.pallas_call(
        functools.partial(opening_kernel, base, count),
        in_specs=[ANY] * 2 + [HBM] * 10,
        out_specs=[VMEM] * 19,
        out_shape=[jax.ShapeDtypeStruct(x.shape, F32),
                   jax.ShapeDtypeStruct((8, 128), F32)] + PREPARED + network_shapes(count),
        scratch_shapes=[pltpu.VMEM((12, 128), F32)] + [pltpu.VMEM((128, 128), F32)] * 3
        + [pltpu.SemaphoreType.DMA((10,))],
        compiler_params=pltpu.CompilerParams(vmem_limit_bytes=LIMIT),
        cost_estimate=cost(count),
        name="network_first",
    )(last, initial, *pinned(x, win, w2, w3, w4, *vectors))


def middle_kernel(base, count, token, x_ref, *rest):
    network_rows(x_ref, base, count, rest[:8], rest[8], rest[9:])


def middle_call(base, count, token, x, prepared, vectors):
    return pl.pallas_call(
        functools.partial(middle_kernel, base, count),
        in_specs=[ANY] + [VMEM] * 10,
        out_specs=[VMEM] * 9,
        out_shape=network_shapes(count),
        compiler_params=pltpu.CompilerParams(vmem_limit_bytes=LIMIT),
        cost_estimate=cost(count),
        name="network",
    )(token, x, *prepared, vectors)


def place(lane, k, offset):
    moved = (lane + offset) & 127
    return (moved >= 8 * k) & (moved < 8 * k + 8)


def packed(up_ref, inv_ref, cpl_ref, mis_ref, down_ref, out_ref, offset):
    rows = mis_ref.shape[1]
    tiles = rows // 8 + 2
    lane = lax.broadcasted_iota(jnp.int32, (8, 128), 1)
    for t in range(tiles):
        for j in range(3):
            out = jnp.zeros((8, 128), F32)
            for k in range(min(16, 46 - 16 * j)):
                value = tile_of(up_ref, inv_ref, cpl_ref, mis_ref, down_ref, 16 * j + k, t)
                here = place(lane, k, offset)
                out = jnp.where(here, pltpu.roll(value, 8 * k, 1) if k else value, out)
            out_ref[j, pl.ds(8 * t, 8)] = out


def tile_of(up_ref, inv_ref, cpl_ref, mis_ref, down_ref, a, t):
    if t == 0:
        return up_ref[a]
    if t == mis_ref.shape[1] // 8 + 1:
        return down_ref[a]
    at = pl.ds(8 * (t - 1), 8)
    if a < 36:
        return inv_ref[a, at]
    return cpl_ref[a - 36, at] if a < 40 else mis_ref[a - 40, at]


def far_kernel(up_ref, inv_ref, cpl_ref, mis_ref, down_ref, token, out_ref):
    packed(up_ref, inv_ref, cpl_ref, mis_ref, down_ref, out_ref, 8 * lax.axis_index("c"))


def far_call(up, inv, cpl, mis, down, token):
    rows = mis.shape[1]
    return pl.pallas_call(
        far_kernel,
        in_specs=[VMEM] * 5 + [ANY],
        out_specs=VMEM,
        out_shape=jax.ShapeDtypeStruct((3, rows + 16, 128), F32),
        compiler_params=pltpu.CompilerParams(vmem_limit_bytes=LIMIT),
        name="far_columns",
    )(up, inv, cpl, mis, down, token)


def third_kernel(base, count, up_ref, inv_ref, cpl_ref, mis_ref, down_ref, x_ref, *rest):
    network_rows(x_ref, base, count, rest[:8], rest[8], rest[10:])
    packed(up_ref, inv_ref, cpl_ref, mis_ref, down_ref, rest[9], 8 - 8 * lax.axis_index("c"))


def third_call(base, count, up, inv, cpl, mis, down, x, prepared, vectors):
    rows = mis.shape[1]
    return pl.pallas_call(
        functools.partial(third_kernel, base, count),
        in_specs=[VMEM] * 15,
        out_specs=[VMEM] * 10,
        out_shape=[jax.ShapeDtypeStruct((3, rows + 16, 128), F32)] + network_shapes(count),
        compiler_params=pltpu.CompilerParams(vmem_limit_bytes=LIMIT),
        cost_estimate=cost(count),
        name="network_near",
    )(up, inv, cpl, mis, down, x, *prepared, vectors)


def final_kernel(up_ref, inv_ref, cpl_ref, mis_ref, down_ref, prod_ref, far_ref, near_ref, wt, *rest):
    parts = [rest[9 * p : 9 * p + 9] for p in range(PARTS)]
    adj_ref, sens_ref, corr_ref, sums_ref, ext, *rest = rest[9 * PARTS :]
    main, side, (acc4, acc3, acc2, acc1, flat) = rest[0:2], rest[2:4], rest[4:]
    rows = mis_ref.shape[1]
    tiles = rows // 8 + 2
    lane = lax.broadcasted_iota(jnp.int32, (8, 128), 1)
    first, last = lane == 0, lane == 127

    def tile(a, t):
        return tile_of(up_ref, inv_ref, cpl_ref, mis_ref, down_ref, a, t)

    offset = 8 * lax.axis_index("c")
    for a in range(46):
        j, k = a // 16, a % 16
        for t in range(tiles):
            at = pl.ds(8 * t, 8)
            both = jnp.where(place(lane, k, offset), near_ref[j, at], far_ref[j, at])
            both = pltpu.roll(both, 128 - 8 * k, 1) if k else both
            ext[a, at] = jnp.where((lane < 8) | (lane >= 120), both, 0.0)

    edge = jnp.zeros((8, 128), F32)
    for field in main + side:
        for i in range(6):
            field[i, 0:8] = edge
            field[i, pl.ds(8 * tiles + 8, 8)] = edge

    def solve(field, t, coefficient, rhs):
        for i in range(6):
            total = coefficient(6 * i) * rhs[0]
            for j in range(1, 6):
                total = total + coefficient(6 * i + j) * rhs[j]
            field[i, pl.ds(8 * t + 8, 8)] = total

    for t in range(tiles):
        at = pl.ds(8 * t, 8)
        solve(main[0], t, lambda a: tile(a, t), [tile(40 + i, t) for i in range(6)])
        solve(side[0], t, lambda a: ext[a, at], [ext[40 + i, at] for i in range(6)])

    def sweep(main, side, main_next, side_next, final=False):
        for t in range(1, tiles - 1) if final else range(tiles):
            at = pl.ds(8 * t, 8)
            near, beside = [], []
            for i in range(6):
                m = main[i, pl.ds(8 * t + 8, 8)]
                e = side[i, pl.ds(8 * t + 8, 8)]
                m_low, m_high = pltpu.roll(m, 1, 1), pltpu.roll(m, 127, 1)
                e_low, e_high = pltpu.roll(e, 1, 1), pltpu.roll(e, 127, 1)
                rhs = tile(40 + i, t) + tile(36, t) * main[i, pl.ds(8 * t + 7, 8)]
                rhs = rhs + tile(37, t) * main[i, pl.ds(8 * t + 9, 8)]
                rhs = rhs + tile(38, t) * jnp.where(first, e_low, m_low)
                near.append(rhs + tile(39, t) * jnp.where(last, e_high, m_high))
                rhs = ext[40 + i, at] + ext[36, at] * side[i, pl.ds(8 * t + 7, 8)]
                rhs = rhs + ext[37, at] * side[i, pl.ds(8 * t + 9, 8)]
                rhs = rhs + ext[38, at] * jnp.where(first, m_low, e_low)
                beside.append(rhs + ext[39, at] * jnp.where(last, m_high, e_high))
            solve(main_next, t, lambda a: tile(a, t), near)
            if not final:
                solve(side_next, t, lambda a: ext[a, at], beside)

    def two(n, carry):
        sweep(main[0], side[0], main[1], side[1])
        sweep(main[1], side[1], main[0], side[0])
        return carry

    lax.fori_loop(0, (SWEEPS - 2) // 2, two, 0)
    if SWEEPS % 2:
        sweep(main[0], side[0], main[1], side[1])
    at = SWEEPS % 2
    sweep(main[at], side[at], main[1 - at], side[1 - at], True)
    done = main[1 - at]

    square = jnp.zeros((8, 128), F32)
    for t in range(rows // 8):
        at = pl.ds(8 * t, 8)
        total = jnp.zeros((8, 128), F32)
        for i in range(6):
            value = done[i, pl.ds(8 * t + 16, 8)]
            adj_ref[i, at] = value
            total = total + value * prod_ref[i, at]
        sens_ref[at] = -total
        square = square + total * total

    for acc in (acc4, acc3, acc2, acc1):
        acc[...] = jnp.zeros_like(acc)
    flat[...] = jnp.zeros_like(flat)

    def term(scaled, right, acc, slot):
        total = flat[slot]
        pieces = []
        for value in scaled:
            total = total + value
            high, low = split(value)
            pieces.append(jnp.concatenate([high, low], axis=0))
        flat[slot] = total
        left = jnp.concatenate(pieces, axis=1)
        acc[...] += jnp.dot(left, right.reshape(128 * len(pieces), right.shape[2]), preferred_element_type=F32)

    base = 0
    for part in parts:
        corr, l1 = part[0], part[2]
        for r in range(corr.shape[0]):
            corr_ref[base + r : base + r + 1] = corr[r]

        def gather(g, carry, base=base, part=part, wide=min(8, l1.shape[0])):
            _, xc, l1, l2, l3, l4t, d3t, d2t, d1t = part
            at = wide * g
            some = pl.ds(at, wide)
            weights = [sens_ref[pl.ds(base + at + r, 1), :] for r in range(wide)]
            out = flat[4]
            scaled = []
            for r in range(wide):
                value = l4t[at + r]
                out = out + value * weights[r]
                scaled.append(wt[...] * (1.0 - value * value) * weights[r])
            flat[4] = out
            term(scaled, l3[some], acc4, 3)
            for delta, layer, acc, slot in ((d3t, l2, acc3, 2), (d2t, l1, acc2, 1), (d1t, xc, acc1, 0)):
                term([delta[at + r] * weights[r] for r in range(wide)], layer[some], acc, slot)
            return carry

        lax.fori_loop(0, l1.shape[0] // min(8, l1.shape[0]), gather, 0)
        base += l1.shape[0]

    for n, acc in enumerate((acc4, acc3, acc2)):
        sums_ref[pl.ds(128 * n, 128)] = (acc[0:128, 0:128] + acc[128:256, 0:128]) + (
            acc[0:128, 128:256] + acc[128:256, 128:256])
    lanes = lax.broadcasted_iota(jnp.int32, (128, 128), 1)
    block = jnp.zeros((128, 128), F32)
    for slot in range(5):
        block = jnp.where(lanes == 16 + slot, jnp.sum(flat[slot], axis=1, keepdims=True), block)
    block = jnp.where(lanes == 21, jnp.sum(square), block)
    own = acc1[0:128] + acc1[128:256]
    own = jnp.concatenate([own, jnp.zeros((128, 80), F32)], axis=1)
    own = own + pltpu.roll(own, 112, 1)
    sums_ref[pl.ds(384, ROWS - 384)] = jnp.where(lanes < 12, own, block).T[0 : ROWS - 384]


def final_call(up, inv, cpl, mis, down, prod, far, near, wt, parts):
    rows = mis.shape[1]
    flat = [value for part in parts for value in part]
    return pl.pallas_call(
        final_kernel,
        in_specs=[VMEM] * (9 + len(flat)),
        out_specs=[VMEM] * 4,
        out_shape=[
            jax.ShapeDtypeStruct((6, rows, 128), F32),
            jax.ShapeDtypeStruct((rows, 128), F32),
            jax.ShapeDtypeStruct((rows, 128), F32),
            jax.ShapeDtypeStruct((ROWS, 128), F32),
        ],
        scratch_shapes=[
            pltpu.VMEM((46, rows + 16, 128), F32),
            pltpu.VMEM((6, rows + 32, 128), F32),
            pltpu.VMEM((6, rows + 32, 128), F32),
            pltpu.VMEM((6, rows + 32, 128), F32),
            pltpu.VMEM((6, rows + 32, 128), F32),
            pltpu.VMEM((256, 256), F32),
            pltpu.VMEM((256, 256), F32),
            pltpu.VMEM((256, 256), F32),
            pltpu.VMEM((256, 48), F32),
            pltpu.VMEM((5, 128, 128), F32),
        ],
        compiler_params=pltpu.CompilerParams(vmem_limit_bytes=2 * LIMIT),
        name="final",
    )(up, inv, cpl, mis, down, prod, far, near, wt, *flat)


def unpack_kernel(sums_ref, w4_ref, w3_ref, w2_ref, win_ref, b1_ref, b2_ref, b3_ref, b4_ref, out_ref):
    scale = 1.0 / jnp.sqrt(sums_ref[405:406] + EPS)
    for n, ref in enumerate((w4_ref, w3_ref, w2_ref)):
        ref[...] = sums_ref[pl.ds(128 * n, 128)] * scale
    win_ref[...] = sums_ref[384:396] * scale
    for n, ref in enumerate((b1_ref, b2_ref, b3_ref, b4_ref, out_ref)):
        ref[...] = sums_ref[400 + n : 401 + n] * scale


def unpack_call(sums):
    shapes = [(128, 128)] * 3 + [(12, 128)] + [(1, 128)] * 5
    return pl.pallas_call(
        unpack_kernel,
        in_specs=[VMEM],
        out_shape=[jax.ShapeDtypeStruct(shape, F32) for shape in shapes],
        compiler_params=pltpu.CompilerParams(vmem_limit_bytes=2 * MIB),
        name="unpack",
    )(sums)


def sent(value, axes, by):
    size = lax.axis_size(axes)
    return lax.ppermute(value, axes, [(i, i + by) for i in range(size) if 0 <= i + by < size])


def swapped(value, start):
    size = lax.axis_size(BLK)
    pairs = [(i, (i + 1) % size) for i in range(start, size, 2)]
    return lax.ppermute(value, BLK, pairs + [(j, i) for i, j in pairs])


def summed(value):
    near, far = lax.axis_size(NEAR), lax.axis_size(FAR)
    piece = (value.shape[0] // near, 1, 128)
    part = lax.all_to_all(value.reshape((near,) + piece), NEAR, 0, 0)
    part = jnp.sum(part, axis=0)
    part = lax.all_to_all(jnp.broadcast_to(part[None], (far,) + piece), FAR, 0, 0)
    part = jnp.sum(part, axis=0)
    whole = lax.all_to_all(jnp.broadcast_to(part[None], (near,) + piece), NEAR, 0, 0)
    return whole.reshape(value.shape)


def local(features, inverse_diag, couplings, mismatch, production, weight_in, bias_in, weight_two,
          bias_two, weight_three, bias_three, weight_four, bias_four, weight_out):
    nvars, rows, cols = mismatch.shape
    inverse = inverse_diag.reshape(nvars * nvars, rows, cols)
    win = weight_in.T
    vectors = [v.reshape(1, 128) for v in (bias_in, bias_two, bias_three, bias_four, weight_out)]
    count = rows // 4

    last, initial = edge_call(inverse, couplings, mismatch)
    above = sent(last, SUB, 1)
    below = sent(initial, SUB, -1)
    features, vectors, *rest = opening_call(
        0, 2 * count, last, initial, features, win, weight_two, weight_three, weight_four, vectors)
    prepared, first = rest[:8], rest[8:]

    far = far_call(above, inverse, couplings, mismatch, below, first[0])
    from_far = swapped(far, 1)
    near, *second = third_call(2 * count, count, above, inverse, couplings, mismatch, below, features,
                               prepared, vectors)
    from_near = swapped(near, 0)
    third = middle_call(3 * count, count, from_far, features, prepared, vectors)

    parts = (first, second, third)
    adjoint, sensitivity, correction, sums = final_call(
        above, inverse, couplings, mismatch, below, production, from_far, from_near, prepared[7],
        parts)
    g4, g3, g2, gin, b1, b2, b3, b4, gout = unpack_call(summed(sums))
    flat = lambda value: value.reshape(128)
    return (adjoint, sensitivity, correction, gin.T, flat(b1), g2, flat(b2),
            g3, flat(b3), g4, flat(b4), flat(gout))


def solution(mesh):
    sizes = (16, 2, 2, 4, 2) if mesh.devices.size == 512 else (mesh.shape["blk"] // 2, 1, 2, mesh.shape["sub"], 1)
    fine = Mesh(mesh.devices.reshape(sizes), BLK + SUB)
    three = P(None, SUB, BLK)
    two = P(SUB, BLK)
    return jax.shard_map(
        local,
        mesh=fine,
        in_specs=(three, P(None, None, SUB, BLK), three, three, three) + (P(),) * 9,
        out_specs=(three, two, two) + (P(),) * 9,
        check_vma=False,
    )
```

```python
import functools
import jax
import jax.numpy as jnp
from jax import lax
from jax.experimental import pallas as pl
from jax.experimental.pallas import tpu as pltpu
from jax.sharding import Mesh, PartitionSpec as P

SWEEPS = 8
EPS = 1e-06
BLK = ("z", "xh", "c")
SUB = ("y", "xl")
NEAR = ("xh", "c", "y", "xl")
FAR = ("z",)
F32 = jnp.float32
BF16 = jnp.bfloat16
GROUP = 8
PARTS = 2
MIB = 1 << 20
ROWS = 416
LIMIT = 8 * MIB


def split(value):
    high = value.astype(BF16)
    return high, (value - high.astype(F32)).astype(BF16)


def pair(value):
    return jnp.concatenate(split(value), axis=1)


def joined(both):
    return both[:, :128].astype(F32) + both[:, 128:].astype(F32)


def times(both, weights):
    out = jnp.dot(both, weights, preferred_element_type=F32)
    return out[:, :128] + out[:, 128:]


def stacked(weight):
    both = pair(weight)
    return jnp.concatenate([both, both], axis=0)


VMEM = pl.BlockSpec(memory_space=pltpu.VMEM)
ANY = pl.BlockSpec(memory_space=pl.ANY)
HBM = pl.BlockSpec(memory_space=pltpu.MemorySpace.HBM)


def network_rows(x_ref, base, count, prepared, vectors, outs):
    s1, f2, f3, f4, b2, b3, b4, wt = prepared
    bias1, bias2, bias3, bias4, wout = (vectors.at[pl.ds(n, 1)] for n in range(5))
    corr_ref, xc_ref, l1_ref, l2_ref, l3_ref, l4t_ref, d3t_ref, d2t_ref, d1t_ref = outs
    pad = jnp.zeros((4, 128), F32)

    def step(g, carry):
        at = GROUP * g
        columns = []
        for r in range(GROUP):
            x = jnp.concatenate([x_ref[:, base + at + r, :], pad], axis=0)
            high = x.astype(BF16).astype(F32)
            column = jnp.concatenate([high, x - high, high], axis=0).T.astype(BF16)
            xc_ref[at + r] = column
            columns.append(column)
        inputs = jnp.concatenate(columns, axis=0)
        layer = jnp.tanh(jnp.dot(inputs, s1[...], preferred_element_type=F32) + bias1[...])
        layers = []
        for out, weights, bias in ((l1_ref, f2, bias2), (l2_ref, f3, bias3), (l3_ref, f4, bias4)):
            layers.append(layer)
            both = pair(layer)
            out[pl.ds(at, GROUP)] = both.reshape(GROUP, 128, 256)
            layer = jnp.tanh(times(both, weights[...]) + bias[...])
        for r in range(GROUP):
            turned = layer[128 * r : 128 * r + 128].T
            l4t_ref[at + r] = turned
            corr_ref[at + r] = 1.0 + jnp.sum(turned * wt[...], axis=0, keepdims=True)
        delta = wout[...] * (1.0 - layer * layer)
        for weights, out in ((b4, d3t_ref), (b3, d2t_ref), (b2, d1t_ref)):
            layer = layers.pop()
            delta = times(pair(delta), weights[...]) * (1.0 - layer * layer)
            for r in range(GROUP):
                out[at + r] = delta[128 * r : 128 * r + 128].T
        return carry

    lax.fori_loop(0, count // GROUP, step, 0)


def network_shapes(count):
    return [
        jax.ShapeDtypeStruct((count, 1, 128), F32),
        jax.ShapeDtypeStruct((count, 128, 48), BF16),
    ] + [jax.ShapeDtypeStruct((count, 128, 256), BF16)] * 3 + [jax.ShapeDtypeStruct((count, 128, 128), F32)] * 4


PREPARED = [jax.ShapeDtypeStruct((48, 128), BF16)] + [jax.ShapeDtypeStruct((256, 256), BF16)] * 6 + [
    jax.ShapeDtypeStruct((128, 128), F32)]


def cost(count):
    return pl.CostEstimate(flops=count * 3 * 10**8, bytes_accessed=count * 1000, transcendentals=0)


def strips(fields, out, row, sem):
    moves, at = [], 0
    for i, field in enumerate(fields):
        n = field.shape[0]
        moves.append(pltpu.make_async_copy(field.at[:, pl.ds(row, 8)], out.at[pl.ds(at, n)], sem.at[i]))
        at += n
    for move in moves:
        move.start()
    return moves


def pinned(*values):
    return [pltpu.with_memory_space_constraint(value, pltpu.MemorySpace.HBM) for value in values]


def edge_kernel(inv_hbm, cpl_hbm, mis_hbm, last, initial, sem):
    rows = mis_hbm.shape[1]
    fields = (inv_hbm, cpl_hbm, mis_hbm)
    moves = strips(fields, last, rows - 8, sem.at[0]) + strips(fields, initial, 0, sem.at[1])
    for move in moves:
        move.wait()


def edge_call(inv, cpl, mis):
    return pl.pallas_call(
        edge_kernel,
        in_specs=[HBM] * 3,
        out_specs=[ANY] * 2,
        out_shape=[jax.ShapeDtypeStruct((46, 8, 128), F32)] * 2,
        scratch_shapes=[pltpu.SemaphoreType.DMA((2, 3))],
        compiler_params=pltpu.CompilerParams(vmem_limit_bytes=MIB),
        name="edge_rows",
    )(*pinned(inv, cpl, mis))


def opening_kernel(base, count, last_hbm, first_hbm, x_hbm, win_hbm, w2_hbm, w3_hbm, w4_hbm, *rest):
    vectors, rest = rest[:5], rest[5:]
    x_ref, vec, prepared, outs = rest[0], rest[1], rest[2:10], rest[10:19]
    win_ref, w2_ref, w3_ref, w4_ref, sem = rest[19:]
    moves = [
        pltpu.make_async_copy(source, target, sem.at[i])
        for i, (source, target) in enumerate(
            [(w2_hbm, w2_ref), (w3_hbm, w3_ref), (w4_hbm, w4_ref), (win_hbm, win_ref), (x_hbm, x_ref)]
            + [(vector, vec.at[pl.ds(n, 1)]) for n, vector in enumerate(vectors)])
    ]
    for move in moves:
        move.start()
    s1, f2, f3, f4, b2, b3, b4, wt = prepared
    for move in moves:
        move.wait()
    win = jnp.concatenate([win_ref[...], jnp.zeros((4, 128), F32)], axis=0)
    high = win.astype(BF16).astype(F32)
    s1[...] = jnp.concatenate([high, high, win - high], axis=0).astype(BF16)
    for raw, ahead, back in ((w2_ref, f2, b2), (w3_ref, f3, b3), (w4_ref, f4, b4)):
        ahead[...] = stacked(raw[...].T)
        back[...] = stacked(raw[...])
    wt[...] = jnp.broadcast_to(vec[4:5], (128, 128)).T
    network_rows(x_ref, base, count, prepared, vec, outs)


def opening_call(base, count, last, initial, x, win, w2, w3, w4, vectors):
    return pl.pallas_call(
        functools.partial(opening_kernel, base, count),
        in_specs=[ANY] * 2 + [HBM] * 10,
        out_specs=[VMEM] * 19,
        out_shape=[jax.ShapeDtypeStruct(x.shape, F32),
                   jax.ShapeDtypeStruct((8, 128), F32)] + PREPARED + network_shapes(count),
        scratch_shapes=[pltpu.VMEM((12, 128), F32)] + [pltpu.VMEM((128, 128), F32)] * 3
        + [pltpu.SemaphoreType.DMA((10,))],
        compiler_params=pltpu.CompilerParams(vmem_limit_bytes=LIMIT),
        cost_estimate=cost(count),
        name="network_first",
    )(last, initial, *pinned(x, win, w2, w3, w4, *vectors))


def middle_kernel(base, count, token, x_ref, *rest):
    network_rows(x_ref, base, count, rest[:8], rest[8], rest[9:])


def middle_call(base, count, token, x, prepared, vectors):
    return pl.pallas_call(
        functools.partial(middle_kernel, base, count),
        in_specs=[ANY] + [VMEM] * 10,
        out_specs=[VMEM] * 9,
        out_shape=network_shapes(count),
        compiler_params=pltpu.CompilerParams(vmem_limit_bytes=LIMIT),
        cost_estimate=cost(count),
        name="network",
    )(token, x, *prepared, vectors)


def place(lane, k, offset):
    moved = (lane + offset) & 127
    return (moved >= 8 * k) & (moved < 8 * k + 8)


def packed(up_ref, inv_ref, cpl_ref, mis_ref, down_ref, out_ref, offset):
    rows = mis_ref.shape[1]
    tiles = rows // 8 + 2
    lane = lax.broadcasted_iota(jnp.int32, (8, 128), 1)
    for t in range(tiles):
        for j in range(3):
            out = jnp.zeros((8, 128), F32)
            for k in range(min(16, 46 - 16 * j)):
                value = tile_of(up_ref, inv_ref, cpl_ref, mis_ref, down_ref, 16 * j + k, t)
                here = place(lane, k, offset)
                out = jnp.where(here, pltpu.roll(value, 8 * k, 1) if k else value, out)
            out_ref[j, pl.ds(8 * t, 8)] = out


def tile_of(up_ref, inv_ref, cpl_ref, mis_ref, down_ref, a, t):
    if t == 0:
        return up_ref[a]
    if t == mis_ref.shape[1] // 8 + 1:
        return down_ref[a]
    at = pl.ds(8 * (t - 1), 8)
    if a < 36:
        return inv_ref[a, at]
    return cpl_ref[a - 36, at] if a < 40 else mis_ref[a - 40, at]


def columns_kernel(far, up_ref, inv_ref, cpl_ref, mis_ref, down_ref, token, out_ref):
    core = lax.axis_index("c")
    packed(up_ref, inv_ref, cpl_ref, mis_ref, down_ref, out_ref, 8 * core if far else 8 - 8 * core)


def columns_call(far, up, inv, cpl, mis, down, token):
    rows = mis.shape[1]
    return pl.pallas_call(
        functools.partial(columns_kernel, far),
        in_specs=[VMEM] * 5 + [ANY],
        out_specs=VMEM,
        out_shape=jax.ShapeDtypeStruct((3, rows + 16, 128), F32),
        compiler_params=pltpu.CompilerParams(vmem_limit_bytes=LIMIT),
        name="far_columns" if far else "near_columns",
    )(up, inv, cpl, mis, down, token)


def mark_kernel(token, mark):
    mark[...] = jnp.zeros_like(mark)


def mark_call(token):
    return pl.pallas_call(
        mark_kernel,
        in_specs=[ANY],
        out_specs=VMEM,
        out_shape=jax.ShapeDtypeStruct((8, 128), F32),
        compiler_params=pltpu.CompilerParams(vmem_limit_bytes=LIMIT),
        name="mark",
    )(token)


def final_kernel(token, up_ref, inv_ref, cpl_ref, mis_ref, down_ref, prod_ref, far_ref, near_ref, wt, *rest):
    parts = [rest[9 * p : 9 * p + 9] for p in range(PARTS)]
    adj_ref, sens_ref, corr_ref, sums_ref, ext, *rest = rest[9 * PARTS :]
    main, side, (acc4, acc3, acc2, acc1, flat) = rest[0:2], rest[2:4], rest[4:]
    rows = mis_ref.shape[1]
    tiles = rows // 8 + 2
    lane = lax.broadcasted_iota(jnp.int32, (8, 128), 1)
    first, last = lane == 0, lane == 127

    def tile(a, t):
        return tile_of(up_ref, inv_ref, cpl_ref, mis_ref, down_ref, a, t)

    offset = 8 * lax.axis_index("c")
    for a in range(46):
        j, k = a // 16, a % 16
        for t in range(tiles):
            at = pl.ds(8 * t, 8)
            both = jnp.where(place(lane, k, offset), near_ref[j, at], far_ref[j, at])
            both = pltpu.roll(both, 128 - 8 * k, 1) if k else both
            ext[a, at] = jnp.where((lane < 8) | (lane >= 120), both, 0.0)

    edge = jnp.zeros((8, 128), F32)
    for field in main + side:
        for i in range(6):
            field[i, 0:8] = edge
            field[i, pl.ds(8 * tiles + 8, 8)] = edge

    def solve(field, t, coefficient, rhs):
        for i in range(6):
            total = coefficient(6 * i) * rhs[0]
            for j in range(1, 6):
                total = total + coefficient(6 * i + j) * rhs[j]
            field[i, pl.ds(8 * t + 8, 8)] = total

    for t in range(tiles):
        at = pl.ds(8 * t, 8)
        solve(main[0], t, lambda a: tile(a, t), [tile(40 + i, t) for i in range(6)])
        solve(side[0], t, lambda a: ext[a, at], [ext[40 + i, at] for i in range(6)])

    def sweep(main, side, main_next, side_next, final=False):
        for t in range(1, tiles - 1) if final else range(tiles):
            at = pl.ds(8 * t, 8)
            near, beside = [], []
            for i in range(6):
                m = main[i, pl.ds(8 * t + 8, 8)]
                e = side[i, pl.ds(8 * t + 8, 8)]
                m_low, m_high = pltpu.roll(m, 1, 1), pltpu.roll(m, 127, 1)
                e_low, e_high = pltpu.roll(e, 1, 1), pltpu.roll(e, 127, 1)
                rhs = tile(40 + i, t) + tile(36, t) * main[i, pl.ds(8 * t + 7, 8)]
                rhs = rhs + tile(37, t) * main[i, pl.ds(8 * t + 9, 8)]
                rhs = rhs + tile(38, t) * jnp.where(first, e_low, m_low)
                near.append(rhs + tile(39, t) * jnp.where(last, e_high, m_high))
                rhs = ext[40 + i, at] + ext[36, at] * side[i, pl.ds(8 * t + 7, 8)]
                rhs = rhs + ext[37, at] * side[i, pl.ds(8 * t + 9, 8)]
                rhs = rhs + ext[38, at] * jnp.where(first, m_low, e_low)
                beside.append(rhs + ext[39, at] * jnp.where(last, m_high, e_high))
            solve(main_next, t, lambda a: tile(a, t), near)
            if not final:
                solve(side_next, t, lambda a: ext[a, at], beside)

    def two(n, carry):
        sweep(main[0], side[0], main[1], side[1])
        sweep(main[1], side[1], main[0], side[0])
        return carry

    lax.fori_loop(0, (SWEEPS - 2) // 2, two, 0)
    if SWEEPS % 2:
        sweep(main[0], side[0], main[1], side[1])
    at = SWEEPS % 2
    sweep(main[at], side[at], main[1 - at], side[1 - at], True)
    done = main[1 - at]

    square = jnp.zeros((8, 128), F32)
    for t in range(rows // 8):
        at = pl.ds(8 * t, 8)
        total = jnp.zeros((8, 128), F32)
        for i in range(6):
            value = done[i, pl.ds(8 * t + 16, 8)]
            adj_ref[i, at] = value
            total = total + value * prod_ref[i, at]
        sens_ref[at] = -total
        square = square + total * total

    for acc in (acc4, acc3, acc2, acc1):
        acc[...] = jnp.zeros_like(acc)
    flat[...] = jnp.zeros_like(flat)

    def term(scaled, right, acc, slot):
        total = flat[slot]
        pieces = []
        for value in scaled:
            total = total + value
            high, low = split(value)
            pieces.append(jnp.concatenate([high, low], axis=0))
        flat[slot] = total
        left = jnp.concatenate(pieces, axis=1)
        acc[...] += jnp.dot(left, right.reshape(128 * len(pieces), right.shape[2]), preferred_element_type=F32)

    base = 0
    for part in parts:
        corr, l1 = part[0], part[2]
        for r in range(corr.shape[0]):
            corr_ref[base + r : base + r + 1] = corr[r]

        def gather(g, carry, base=base, part=part, wide=min(8, l1.shape[0])):
            _, xc, l1, l2, l3, l4t, d3t, d2t, d1t = part
            at = wide * g
            some = pl.ds(at, wide)
            weights = [sens_ref[pl.ds(base + at + r, 1), :] for r in range(wide)]
            out = flat[4]
            scaled = []
            for r in range(wide):
                value = l4t[at + r]
                out = out + value * weights[r]
                scaled.append(wt[...] * (1.0 - value * value) * weights[r])
            flat[4] = out
            term(scaled, l3[some], acc4, 3)
            for delta, layer, acc, slot in ((d3t, l2, acc3, 2), (d2t, l1, acc2, 1), (d1t, xc, acc1, 0)):
                term([delta[at + r] * weights[r] for r in range(wide)], layer[some], acc, slot)
            return carry

        lax.fori_loop(0, l1.shape[0] // min(8, l1.shape[0]), gather, 0)
        base += l1.shape[0]

    for n, acc in enumerate((acc4, acc3, acc2)):
        sums_ref[pl.ds(128 * n, 128)] = (acc[0:128, 0:128] + acc[128:256, 0:128]) + (
            acc[0:128, 128:256] + acc[128:256, 128:256])
    lanes = lax.broadcasted_iota(jnp.int32, (128, 128), 1)
    block = jnp.zeros((128, 128), F32)
    for slot in range(5):
        block = jnp.where(lanes == 16 + slot, jnp.sum(flat[slot], axis=1, keepdims=True), block)
    block = jnp.where(lanes == 21, jnp.sum(square), block)
    own = acc1[0:128] + acc1[128:256]
    own = jnp.concatenate([own, jnp.zeros((128, 80), F32)], axis=1)
    own = own + pltpu.roll(own, 112, 1)
    sums_ref[pl.ds(384, ROWS - 384)] = jnp.where(lanes < 12, own, block).T[0 : ROWS - 384]


def final_call(token, up, inv, cpl, mis, down, prod, far, near, wt, parts):
    rows = mis.shape[1]
    flat = [value for part in parts for value in part]
    return pl.pallas_call(
        final_kernel,
        in_specs=[VMEM] * (10 + len(flat)),
        out_specs=[VMEM] * 4,
        out_shape=[
            jax.ShapeDtypeStruct((6, rows, 128), F32),
            jax.ShapeDtypeStruct((rows, 128), F32),
            jax.ShapeDtypeStruct((rows, 128), F32),
            jax.ShapeDtypeStruct((ROWS, 128), F32),
        ],
        scratch_shapes=[
            pltpu.VMEM((46, rows + 16, 128), F32),
            pltpu.VMEM((6, rows + 32, 128), F32),
            pltpu.VMEM((6, rows + 32, 128), F32),
            pltpu.VMEM((6, rows + 32, 128), F32),
            pltpu.VMEM((6, rows + 32, 128), F32),
            pltpu.VMEM((256, 256), F32),
            pltpu.VMEM((256, 256), F32),
            pltpu.VMEM((256, 256), F32),
            pltpu.VMEM((256, 48), F32),
            pltpu.VMEM((5, 128, 128), F32),
        ],
        compiler_params=pltpu.CompilerParams(vmem_limit_bytes=2 * LIMIT),
        name="final",
    )(token, up, inv, cpl, mis, down, prod, far, near, wt, *flat)


def unpack_kernel(sums_ref, w4_ref, w3_ref, w2_ref, win_ref, b1_ref, b2_ref, b3_ref, b4_ref, out_ref):
    scale = 1.0 / jnp.sqrt(sums_ref[405:406] + EPS)
    for n, ref in enumerate((w4_ref, w3_ref, w2_ref)):
        ref[...] = sums_ref[pl.ds(128 * n, 128)] * scale
    win_ref[...] = sums_ref[384:396] * scale
    for n, ref in enumerate((b1_ref, b2_ref, b3_ref, b4_ref, out_ref)):
        ref[...] = sums_ref[400 + n : 401 + n] * scale


def unpack_call(sums):
    shapes = [(128, 128)] * 3 + [(12, 128)] + [(1, 128)] * 5
    return pl.pallas_call(
        unpack_kernel,
        in_specs=[VMEM],
        out_shape=[jax.ShapeDtypeStruct(shape, F32) for shape in shapes],
        compiler_params=pltpu.CompilerParams(vmem_limit_bytes=2 * MIB),
        name="unpack",
    )(sums)


def sent(value, axes, by):
    size = lax.axis_size(axes)
    return lax.ppermute(value, axes, [(i, i + by) for i in range(size) if 0 <= i + by < size])


def swapped(value, start):
    size = lax.axis_size(BLK)
    pairs = [(i, (i + 1) % size) for i in range(start, size, 2)]
    return lax.ppermute(value, BLK, pairs + [(j, i) for i, j in pairs])


def summed(value):
    near, far = lax.axis_size(NEAR), lax.axis_size(FAR)
    piece = (value.shape[0] // near, 1, 128)
    part = lax.all_to_all(value.reshape((near,) + piece), NEAR, 0, 0)
    part = jnp.sum(part, axis=0)
    part = lax.all_to_all(jnp.broadcast_to(part[None], (far,) + piece), FAR, 0, 0)
    part = jnp.sum(part, axis=0)
    whole = lax.all_to_all(jnp.broadcast_to(part[None], (near,) + piece), NEAR, 0, 0)
    return whole.reshape(value.shape)


def local(features, inverse_diag, couplings, mismatch, production, weight_in, bias_in, weight_two,
          bias_two, weight_three, bias_three, weight_four, bias_four, weight_out):
    nvars, rows, cols = mismatch.shape
    inverse = inverse_diag.reshape(nvars * nvars, rows, cols)
    win = weight_in.T
    vectors = [v.reshape(1, 128) for v in (bias_in, bias_two, bias_three, bias_four, weight_out)]
    count = 8 * (rows * 3 // 32)

    last, initial = edge_call(inverse, couplings, mismatch)
    above = sent(last, SUB, 1)
    below = sent(initial, SUB, -1)
    features, vectors, *rest = opening_call(
        0, count, last, initial, features, win, weight_two, weight_three, weight_four, vectors)
    prepared, first = rest[:8], rest[8:]

    far = columns_call(True, above, inverse, couplings, mismatch, below, first[0])
    from_far = swapped(far, 1)
    near = columns_call(False, above, inverse, couplings, mismatch, below, far)
    from_near = swapped(near, 0)
    second = middle_call(count, rows - count, near, features, prepared, vectors)
    adjoint, sensitivity, correction, sums = final_call(
        mark_call(from_far), above, inverse, couplings, mismatch, below, production, from_far, from_near,
        prepared[7], (first, second))
    g4, g3, g2, gin, b1, b2, b3, b4, gout = unpack_call(summed(sums))
    flat = lambda value: value.reshape(128)
    return (adjoint, sensitivity, correction, gin.T, flat(b1), g2, flat(b2),
            g3, flat(b3), g4, flat(b4), flat(gout))


def solution(mesh):
    sizes = (16, 2, 2, 4, 2) if mesh.devices.size == 512 else (mesh.shape["blk"] // 2, 1, 2, mesh.shape["sub"], 1)
    fine = Mesh(mesh.devices.reshape(sizes), BLK + SUB)
    three = P(None, SUB, BLK)
    two = P(SUB, BLK)
    return jax.shard_map(
        local,
        mesh=fine,
        in_specs=(three, P(None, None, SUB, BLK), three, three, three) + (P(),) * 9,
        out_specs=(three, two, two) + (P(),) * 9,
        check_vma=False,
    )
```
